256 devices in a mesh: inst: 8 (over z_lo, core), tp: 32 (over x, y, z_hi).
Axes of the slice: x: 4, y: 4, z: 8 (z_hi: 2, z_lo: 4; z = z_hi * 4 + z_lo), core: 2. Of those that a mesh axis runs over, the one named last changes fastest.
Arguments:
- queries: bfloat16 [32, 8192], P('inst', 'tp')
- new_kv: bfloat16 [32, 2048], P('inst'), may hold values from -6 to 6
- kv_cache: bfloat16 [32, 4096, 2048], P('inst', 'tp')
- lengths: int32 [32], replicated, may hold values from 2 to 4096, as said below
- move_from: int32 [32], replicated, may hold values from 0 to 31, as said below
- o_weight: bfloat16 [8192, 8192], P('tp'), may hold values from -0.125 to 0.125
Outputs:
- attended: bfloat16 [32, 8192], P('inst', 'tp')
- new_cache: bfloat16 [32, 4096, 2048], P('inst', 'tp')
The draws below stay inside these ranges and needn't reach their ends.
Inputs may be any that keep to these rules, and one draw needn't show every extreme that they name: `move_from`: a permutation of the 32 requests; slot g lies on instance g // 4; 3 requests leave each instance and 3 arrive at each, each from a different instance, so that from one instance to one other instance at most one request moves. `lengths`: some request has length 2 and some the full 4096.
All inputs are finite; a program needn't handle non-finite values.
Results may differ from the reference program's by a relative error of at most 0.0051.
Values may be sent and summed in bfloat16 or wider, within the bound.
A program may use at most 64 MiB of HBM per device.

```python
import jax
import jax.numpy as jnp
from jax import lax

D = 8192
QH = 64
KVH = 8
HD = 128
REQ = 4
PART = 128
REQS = 32
LEN = 4096
MOVES = 3
N_INST = 8
N_TP = 32


def first_keys(key):
    inner = jax.random.fold_in(key, 901)
    return jnp.clip(jax.random.normal(inner, (REQS, KVH * HD), jnp.float32), -6.0, 6.0)


def migration_table(key):
    inner = jax.random.fold_in(key, 902)
    key_relabel, key_steps, key_slots, key_order = jax.random.split(inner, 4)
    instances = jnp.arange(N_INST, dtype=jnp.int32)
    relabel = jax.random.permutation(key_relabel, N_INST).astype(jnp.int32)
    rank = jnp.zeros((N_INST,), jnp.int32).at[relabel].set(instances)
    steps = (1 + jax.random.permutation(key_steps, N_INST - 1)).astype(jnp.int32)
    placed = jax.vmap(lambda number: jax.random.permutation(jax.random.fold_in(key_slots, number), REQ))(instances).astype(jnp.int32)
    ordered = jax.vmap(lambda number: jax.random.permutation(jax.random.fold_in(key_order, number), REQ))(instances).astype(jnp.int32)
    position = jnp.arange(REQ, dtype=jnp.int32)[None, :]
    step_at = steps[jnp.minimum(position, N_INST - 2)]
    remote = relabel[(rank[:, None] - step_at) % N_INST]
    sources = jnp.where(position < MOVES, remote, instances[:, None]).astype(jnp.int32)
    taken = sources * REQ + ordered[sources, jnp.broadcast_to(position, sources.shape)]
    targets = instances[:, None] * REQ + placed
    return jnp.zeros((REQS,), jnp.int32).at[targets.reshape(-1)].set(taken.reshape(-1).astype(jnp.int32))


def draw_move_from(key, part):
    return migration_table(key)


def draw_lengths(key, part):
    key = jax.random.fold_in(key, 3)
    key_len, key_pick = jax.random.split(key)
    drawn = jax.random.randint(key_len, (REQS,), 2, LEN + 1).astype(jnp.int32)
    chosen = jax.random.randint(key_pick, (), 0, REQS)
    return drawn.at[chosen].set(LEN).at[(chosen + 1) % REQS].set(2)


def draw_kv_cache(key, part):
    shared = first_keys(key)
    key = jax.random.fold_in(key, 1)
    shape = (REQS, LEN, 2 * KVH * HD)
    base = jnp.clip(jax.random.normal(key, shape, jnp.float32), -6.0, 6.0)
    base = base.at[:, 0, :KVH * HD].set(shared)
    return base.astype(jnp.bfloat16)


def draw_queries(key, part):
    key = jax.random.fold_in(key, 2)
    base = jnp.clip(jax.random.normal(key, (REQS, QH, HD), jnp.float32), -6.0, 6.0)
    return base.reshape(REQS, QH * HD).astype(jnp.bfloat16)


def spiked(values, stream_key, source, target, blocks, factor):
    owner, partner = [(jnp.arange(values.shape[dim]) // (values.shape[dim] // blocks)).reshape([-1 if axis == dim else 1 for axis in range(values.ndim)]) for dim in (source, target)]
    chosen = jax.random.permutation(stream_key, blocks)[partner]
    strong = (owner == chosen) | (owner == (partner + blocks // 2) % blocks)
    return jnp.where(strong, factor * values, values)


def shard_levels(stream_key, shape, shards, least, high):
    def one(axis_at, shards_of):
        draws = jax.random.uniform(jax.random.fold_in(jax.random.fold_in(stream_key, 6), axis_at), (shards_of,), jnp.float32, least / len(shards), high / len(shards))
        return jnp.repeat(jnp.exp(draws), shape[axis_at] // shards_of).reshape((-1,) + (1,) * (len(shape) - axis_at - 1))

    loudness = one(*shards[0])
    for cut in shards[1:]:
        loudness = loudness * one(*cut)
    return loudness


def bell_draw(rng, extent, scale, reach, cuts=(), kind=jnp.bfloat16):
    entries = jax.random.normal(rng, extent, jnp.float32) * scale
    if len(cuts) > 0:
        entries = shard_levels(rng, extent, cuts, -0.22, 0.18) * entries
    return jnp.clip(entries, min=-reach, max=reach).astype(kind)


def bell_draw_with(key, dims, spread, bound, cuts, heavy, kind=jnp.bfloat16):
    array = spread * jax.random.normal(key, dims, jnp.float32)
    if cuts:
        array = array * shard_levels(key, dims, cuts, -0.22, 0.18)
    return jnp.clip(spiked(array, jax.random.fold_in(key, 3), *heavy), -bound, bound).astype(kind)


def setup_inputs(seed: int = 0) -> dict:
    splits = jax.random.split(jax.random.key(seed), 7)
    queries = draw_queries(jax.random.fold_in(splits[6], 71), 0)
    new_kv = bell_draw(splits[1], (REQS, 2 * KVH * HD), 1.0, 6.0, ((0, 8),))
    kv_cache = draw_kv_cache(jax.random.fold_in(splits[6], 71), 0)
    lengths = draw_lengths(jax.random.fold_in(splits[6], 71), 0)
    move_from = draw_move_from(jax.random.fold_in(splits[6], 71), 0)
    o_weight = bell_draw_with(splits[5], (QH * HD, D), (QH * HD) ** -0.5, 0.125, ((0, 32),), (0, 1, 32, 2.75))
    return dict(queries=queries, new_kv=new_kv, kv_cache=kv_cache, lengths=lengths, move_from=move_from, o_weight=o_weight)


def block_attention(bundle):
    query_row, new_row, cache_rows, seq_length = bundle
    group_size = QH // KVH
    kv_width = KVH * HD
    score_scale = HD ** -0.5
    key_blocks = cache_rows[:, :kv_width].reshape(N_TP, PART, KVH, HD).astype(jnp.float32)
    value_blocks = cache_rows[:, kv_width:].reshape(N_TP, PART, KVH, HD).astype(jnp.float32)
    query_heads = query_row.reshape(KVH, group_size, HD).astype(jnp.float32)
    scores = jnp.einsum("hgd,bphd->bhgp", query_heads, key_blocks) * score_scale
    positions = (jnp.arange(N_TP, dtype=jnp.int32)[:, None] * PART + jnp.arange(PART, dtype=jnp.int32)[None, :]).astype(jnp.int32)
    usable = (positions < seq_length)[:, None, None, :]
    masked = jnp.where(usable, scores, -1e30)
    block_max = jnp.max(masked, axis=-1)
    weights = jnp.where(usable, jnp.exp(masked - block_max[..., None]), 0.0)
    block_total = jnp.sum(weights, axis=-1)
    rounded = lax.optimization_barrier(weights.astype(jnp.bfloat16)).astype(jnp.float32)
    block_sum = jnp.einsum("bhgp,bphd->bhgd", rounded, value_blocks)
    overall = jnp.max(block_max, axis=0)
    factor = jnp.exp(block_max - overall)
    total_all = jnp.sum(block_total * factor, axis=0)
    summed_all = jnp.sum(block_sum * factor[..., None], axis=0)
    new_keys = new_row[:kv_width].reshape(KVH, HD).astype(jnp.float32)
    new_values = new_row[kv_width:].reshape(KVH, HD).astype(jnp.float32)
    own_score = jnp.einsum("hgd,hd->hg", query_heads, new_keys) * score_scale
    highest = jnp.maximum(overall, own_score)
    old_part = jnp.exp(overall - highest)
    new_part = jnp.exp(own_score - highest)
    result = (summed_all * old_part[..., None] + new_part[..., None] * new_values[:, None, :]) / (total_all * old_part + new_part)[..., None]
    return result.reshape(QH * HD).astype(jnp.bfloat16)


def reference(queries, new_kv, kv_cache, lengths, move_from, o_weight):
    moved = jnp.take(kv_cache, move_from, axis=0)
    seq_lengths = jnp.take(lengths, move_from)
    attention = lax.map(block_attention, (queries, new_kv, moved, seq_lengths))
    attended = jnp.dot(attention, o_weight, preferred_element_type=jnp.float32).astype(jnp.bfloat16)
    return attended, moved
```

```python
import functools

import jax
import jax.numpy as jnp
from jax import lax
from jax.experimental import pallas as pl
from jax.experimental.pallas import tpu as pltpu
from jax.sharding import PartitionSpec as P

MESH = pl.DeviceIdType.MESH
KVH = 8
HD = 128
SCALE = HD ** -0.5
STEPS = (6, 7, 8, 9, 12)
PIECES = 4
ROWS = 16
F32 = jnp.float32
BF16 = jnp.bfloat16

SEND, PLACE, SLOT_OF, LENGTH, SOURCE, ONCHIP, DUMP = 0, 32, 40, 44, 48, 52, 63


def plan_kernel(move_ref, len_ref, tab_ref, pick_ref, slot_of, count, rank, par, free):
    inst = lax.axis_index("inst")
    chip = inst // 2
    for n in range(64):
        tab_ref[n] = 0
    for n in range(32):
        tab_ref[SEND + n] = -1
        slot_of[move_ref[n]] = n
    for n in range(16):
        count[n] = 0
    for r in range(32):
        kind = (r // 8) * 4 + lax.shift_right_logical(slot_of[r], 3)
        seen = count[kind]
        rank[r] = seen
        count[kind] = seen + 1
    most = jnp.int32(STEPS[0])
    for d in range(2):

        def number(a, b):
            return count[a * 4 + b] if d == 0 else count[(3 - a) * 4 + 3 - b]

        n02, n03, n12, n13 = number(0, 2), number(0, 3), number(1, 2), number(1, 3)
        o0, o1 = n02 + n03, n12 + n13
        par[d * 8 + 0] = n03
        par[d * 8 + 1] = o0
        par[d * 8 + 2] = n13
        one = jnp.int32(1)
        mask = lax.shift_left(lax.shift_left(one, n03) - 1, jnp.int32(2))
        again = lax.shift_left(lax.shift_left(one, jnp.maximum(n13 - 1, 0)) - 1, o0 + 2)
        mask = mask | jnp.where(n13 > 0, again | 2, 0)
        seen = jnp.int32(0)
        for s in range(10):
            free[d * 16 + seen] = s
            seen = seen + 1 - (lax.shift_right_logical(mask, jnp.int32(s)) & 1)
        most = jnp.maximum(most, o0 + jnp.maximum(o1, jnp.minimum(o0, 1)))
        most = jnp.maximum(most, jnp.where(n13 > 1, o0 + n13 + 1, 0))
    pick = jnp.int32(0)
    for steps in STEPS[:-1]:
        pick = pick + (most > steps).astype(jnp.int32)
    pick_ref[0] = pick

    def first_step(r, a_chip, b_chip):
        d = (b_chip < a_chip).astype(jnp.int32)
        a = jnp.where(d == 1, 3 - a_chip, a_chip)
        b = jnp.where(d == 1, 3 - b_chip, b_chip)
        k = rank[r]
        n03, o0, n13 = par[d * 8], par[d * 8 + 1], par[d * 8 + 2]
        p0 = k + jnp.where(b == 3, 0, jnp.where(b == 2, n03, o0))
        q = jnp.where(b == 3, k, n13 + k)
        p1 = jnp.where(q == 0, 0, o0 + q)
        p2 = free[d * 16 + k]
        return d, jnp.where(a == 0, p0, jnp.where(a == 1, p1, p2)), b - a

    for q in range(8):
        r = chip * 8 + q
        b = lax.shift_right_logical(slot_of[r], 3)
        d, step, _ = first_step(r, chip, b)
        tab_ref[jnp.where(b == chip, DUMP, SEND + d * 16 + step)] = q
    for k in range(4):
        r = inst * 4 + k
        g = slot_of[r]
        home = lax.shift_right_logical(g, 2)
        tab_ref[jnp.where((home != inst) & (home // 2 == chip), ONCHIP, DUMP)] = k
        tab_ref[SLOT_OF + k] = g
        tab_ref[LENGTH + k] = len_ref[r]
    for j in range(4):
        r = move_ref[inst * 4 + j]
        home = lax.shift_right_logical(r, 2)
        a = lax.shift_right_logical(r, 3)
        d, step, hops = first_step(r, a, chip)
        arrival = 8 + d * 16 + step + hops - 1
        tab_ref[PLACE + j] = jnp.where(home == inst, r & 3, jnp.where(a == chip, 4, arrival))
        tab_ref[SOURCE + j] = r


def main_kernel(
    steps, tab, q_ref, new_ref, cache, weight, attended, arrived, onchip,
    own, part, tx, rx, on_stage, w_buf,
    a_send, a_buf, b_send, b_buf, d_send, d_buf, e_send, e_buf, h_send, h_buf, i_send, i_buf, j_send, j_buf,
    tx_sem, rx_sem, mir_send, mir_recv, keep_sem, part_send, part_recv, on_sem, load_sem,
    a_ss, a_rs, b_ss, b_rs, d_ss, d_rs, e_sem, h_ss, h_rs, i_sem, j_ss, j_rs,
):
    inst = lax.axis_index("inst")
    tp = lax.axis_index("tp")
    chip, core = inst // 2, inst % 2
    zh, u = tp % 2, tp // 2
    me = zh * 8 + inst
    partner = {"inst": chip * 2 + 1 - core}
    z_partner = {"tp": u * 2 + 1 - zh}

    def peer16(d):
        e = (me + d) % 16
        return {"inst": e % 8, "tp": u * 2 + e // 8}

    def peer_xy(d):
        return {"tp": ((u + d) % 16) * 2 + zh}

    def remote(src, dst, ss, rs, to):
        return pltpu.make_async_remote_copy(
            src_ref=src, dst_ref=dst, send_sem=ss, recv_sem=rs, device_id=to, device_id_type=MESH
        )

    half = pl.multiple_of(core * 64, 64)
    other = pl.multiple_of(64 - core * 64, 64)
    loads = [
        pltpu.make_async_copy(cache, own, load_sem.at[0]),
        pltpu.make_async_copy(weight, w_buf, load_sem.at[1]),
    ]
    for load in loads:
        load.start()

    barrier = pltpu.get_barrier_semaphore()
    for d in range(1, 16):
        pl.semaphore_signal(barrier, inc=1, device_id=peer16(d), device_id_type=MESH)
        pl.semaphore_signal(barrier, inc=1, device_id=peer_xy(d), device_id_type=MESH)
    pl.semaphore_wait(barrier, 30)

    shares = [
        remote(
            cache.at[:, pl.ds(pl.multiple_of(other + p * ROWS, ROWS), ROWS)],
            part[p], part_send.at[p], part_recv.at[p], partner,
        )
        for p in range(PIECES)
    ]
    for share in shares:
        share.start()

    def has_in(d):
        return chip > 0 if d == 0 else chip < 3

    def has_out(d):
        return chip < 3 if d == 0 else chip > 0

    def hop(d, s, p):
        to = {"inst": jnp.clip(inst + (2 if d == 0 else -2), 0, 7)}
        rows = pl.ds(p * ROWS, ROWS)
        return remote(tx.at[d, s, rows], rx.at[d, s, rows], tx_sem.at[d, s, p], rx_sem.at[d, s, p], to)

    def mirror(d, s, p0, count):
        rows = pl.ds(p0 * ROWS, count * ROWS)
        there = pl.ds(pl.multiple_of(half + p0 * ROWS, ROWS), count * ROWS)
        src = rx.at[d, s, rows]
        dst = arrived.at[d, s, there]
        return (
            remote(src, dst, mir_send.at[d, s, p0], mir_recv.at[d, s, p0], partner),
            pltpu.make_async_copy(src, dst, keep_sem.at[d, s, p0]),
        )

    def migrate(s, p, first):
        rows = pl.ds(p * ROWS, ROWS)
        if first:
            shares[p].wait_recv()
        own_rows = pl.ds(pl.multiple_of(half + p * ROWS, ROWS), ROWS)
        for d in range(2):
            if not first:

                @pl.when(has_in(d))
                def _():
                    hop(d, s - 1, p).wait_recv()

            @pl.when(has_out(d))
            def _():
                code = tab[SEND + d * 16 + s]
                choice = jnp.maximum(code, 0)
                mine = lax.shift_right_logical(choice, 2) == core
                index = choice & 3
                block = jnp.where(mine, own[index, own_rows, :], part[p][index])
                if not first:
                    block = jnp.where(code < 0, rx[d, s - 1, rows, :], block)
                tx[d, s, rows, :] = block
                hop(d, s, p).start()

            if not first and p == PIECES - 1:

                @pl.when(has_in(d))
                def _():
                    for copy in mirror(d, s - 1, 0, PIECES):
                        copy.start()

    def end_piece(p):
        for d in range(2):

            @pl.when(has_in(d))
            def _():
                hop(d, steps - 1, p).wait_recv()
                for copy in mirror(d, steps - 1, p, 1):
                    copy.start()

    row16 = lax.broadcasted_iota(jnp.int32, (16, 1), 0)

    def by_slot(kind, values):
        out = jnp.full(kind.shape, values[0], jnp.int32)
        for k in range(1, 4):
            out = jnp.where(kind == k, values[k], out)
        return out

    def a_copy(d):
        return remote(a_send, a_buf.at[me], a_ss.at[d - 1], a_rs.at[d - 1], peer16(d))

    def a_take(d):
        return remote(a_send, a_buf.at[(me + 16 - d) % 16], a_ss.at[d - 1], a_rs.at[d - 1], peer16(d))

    def stage_a():
        lanes = pl.ds(pl.multiple_of((u // 2) * HD, HD), HD)
        value_lanes = pl.ds(pl.multiple_of(KVH * HD + (u // 2) * HD, HD), HD)
        q = q_ref[...].astype(F32)
        packed = jnp.concatenate(
            [q[:, :HD], q[:, HD:], new_ref[:, lanes].astype(F32), new_ref[:, value_lanes].astype(F32)], axis=0
        ).astype(BF16)
        a_send[...] = packed
        a_buf[pl.ds(me, 1)] = packed[None]
        for d in range(1, 16):
            a_copy(d).start()

    def xy_copy(send, buf, ss, rs, d, whole):
        src = send if whole else send.at[(u + d) % 16]
        return remote(src, buf.at[u], ss.at[d - 1], rs.at[d - 1], peer_xy(d))

    def xy_take(send, buf, ss, rs, d, whole):
        src = send if whole else send.at[(u + d) % 16]
        return remote(src, buf.at[(u + 16 - d) % 16], ss.at[d - 1], rs.at[d - 1], peer_xy(d))

    def stage_b():
        for d in range(1, 16):
            a_take(d).wait_recv()
        blocks, spots = [], []
        for k in range(4):
            g = tab[SLOT_OF + k]
            spots.append(g & 3)
            for z in range(2):
                blocks.append(a_buf[z * 8 + lax.shift_right_logical(g, 2)])
        stacked = jnp.concatenate(blocks, axis=0)
        row = lax.broadcasted_iota(jnp.int32, (48, 128), 0)
        col = lax.broadcasted_iota(jnp.int32, (48, 128), 1)
        inner = row % 16
        k, h, group = inner // 4, inner % 4, row // 16
        spot = by_slot(k, spots)
        place = jnp.where(
            group == 0, (k * 2 + h // 2) * 16 + (h % 2) * 4, k * 32 + 4 + group * 4
        )
        chosen = (col == place + spot).astype(F32).astype(BF16)
        picked = jnp.dot(chosen, stacked, preferred_element_type=F32)
        mine = picked[:16].astype(BF16)
        b_send[...] = mine
        b_buf[pl.ds(u, 1)] = mine[None]
        for d in range(1, 16):
            xy_copy(b_send, b_buf, b_ss, b_rs, d, True).start()
        return picked

    def wait_b():
        for d in range(1, 16):
            xy_take(b_send, b_buf, b_ss, b_rs, d, True).wait_recv()

    row32 = lax.broadcasted_iota(jnp.int32, (32, 1), 0)
    of_row = (row32 % 16) // 4

    def stage_c(heads):
        limit = by_slot(of_row, [tab[LENGTH + k] for k in range(4)])
        position = tp * 128 + lax.broadcasted_iota(jnp.int32, (32, 128), 1)
        usable = position < limit
        for k in heads:
            query = b_buf[2 * k : 2 * k + 2].reshape(32, HD)
            keys = own[:, :, k * HD : (k + 1) * HD].reshape(512, HD)
            values = own[:, :, (KVH + k) * HD : (KVH + k + 1) * HD].reshape(512, HD)
            full = lax.dot_general(query, keys, (((1,), (1,)), ((), ())), preferred_element_type=F32)
            scores = full[:, :128]
            for r in range(1, 4):
                scores = jnp.where(of_row == r, full[:, r * 128 : (r + 1) * 128], scores)
            masked = jnp.where(usable, scores * SCALE, -1e30)
            top = jnp.max(masked, axis=1, keepdims=True)
            weights = jnp.where(usable, jnp.exp(masked - top), 0.0)
            total = jnp.sum(weights, axis=1, keepdims=True)
            spread = jnp.concatenate(
                [jnp.where(of_row == r, weights, 0.0).astype(BF16) for r in range(4)], axis=1
            )
            summed = jnp.dot(spread, values, preferred_element_type=F32)
            lane = lax.broadcasted_iota(jnp.int32, (32, HD), 1)
            stats = jnp.where(lane < 64, top, total)
            d_send[2 * k : 2 * k + 2] = jnp.concatenate([summed, stats], axis=1).reshape(2, 16, 2 * HD)

    def send_d():
        d_buf[pl.ds(u, 1)] = d_send[pl.ds(u, 1)]
        for d in range(1, 16):
            xy_copy(d_send, d_buf, d_ss, d_rs, d, False).start()

    def merge(blocks):
        tops = [block[:, HD : HD + 1] for block in blocks]
        top = functools.reduce(jnp.maximum, tops)
        factors = [jnp.exp(t - top) for t in tops]
        summed = sum(block[:, :HD] * f for block, f in zip(blocks, factors))
        total = sum(block[:, HD + 64 : HD + 65] * f for block, f in zip(blocks, factors))
        return top, total, summed

    def e_copy():
        return remote(e_send, e_buf, e_sem.at[0], e_sem.at[1], z_partner)

    def stage_d():
        for d in range(1, 16):
            xy_take(d_send, d_buf, d_ss, d_rs, d, False).wait_recv()
        top, total, summed = merge([d_buf[n] for n in range(16)])
        lane = lax.broadcasted_iota(jnp.int32, (16, HD), 1)
        e_send[...] = jnp.concatenate([summed, jnp.where(lane < 64, top, total)], axis=1)
        e_copy().start()

    def stage_e(picked):
        e_copy().wait_recv()
        top, total, summed = merge([e_send[...], e_buf[...]])
        query, key, value = picked[:16], picked[16:32], picked[32:48]
        own_score = jnp.sum(query * key, axis=1, keepdims=True) * SCALE
        highest = jnp.maximum(top, own_score)
        old, new = jnp.exp(top - highest), jnp.exp(own_score - highest)
        attention = ((summed * old + new * value) / (total * old + new)).astype(BF16)
        row = lax.broadcasted_iota(jnp.int32, (16, 16), 0)
        col = lax.broadcasted_iota(jnp.int32, (16, 16), 1)
        heads = []
        for h in range(2):
            chosen = ((col == (row % 4) * 4 + zh * 2 + h) & (row < 8)).astype(F32).astype(BF16)
            heads.append(jnp.dot(chosen, attention, preferred_element_type=F32))
        both = jnp.concatenate(heads, axis=1)
        low = jnp.where(row16 < 4, both, 0.0).astype(BF16)
        high = jnp.where(row16 >= 4, both, 0.0).astype(BF16)
        return low, high

    def stage_f(low, high, first, last):
        for n in range(first, last):
            at = n * 512
            out = jnp.dot(low, w_buf[:, at : at + 256], preferred_element_type=F32)
            out = out + jnp.dot(high, w_buf[:, at + 256 : at + 512], preferred_element_type=F32)
            h_send[n] = out[:8]

    def send_h():
        h_buf[pl.ds(u, 1)] = h_send[pl.ds(u, 1)]
        for d in range(1, 16):
            xy_copy(h_send, h_buf, h_ss, h_rs, d, False).start()

    def i_copy():
        return remote(i_send, i_buf, i_sem.at[0], i_sem.at[1], z_partner)

    def stage_h():
        for d in range(1, 16):
            xy_take(h_send, h_buf, h_ss, h_rs, d, False).wait_recv()
        i_send[...] = sum(h_buf[n] for n in range(16))
        i_copy().start()

    def j_copy(d):
        return remote(j_send, j_buf.at[inst], j_ss.at[d - 1], j_rs.at[d - 1], {"inst": (inst + d) % 8})

    def j_take(d):
        return remote(
            j_send, j_buf.at[(inst + 8 - d) % 8], j_ss.at[d - 1], j_rs.at[d - 1], {"inst": (inst + d) % 8}
        )

    def stage_i():
        i_copy().wait_recv()
        total = i_send[...] + i_buf[...]
        total = jnp.where(zh == 0, total[:4], total[4:])
        packed = jnp.concatenate([total[:, :HD], total[:, HD:]], axis=0)
        j_send[...] = packed
        j_buf[pl.ds(inst, 1)] = packed[None]
        for d in range(1, 8):
            j_copy(d).start()

    def stage_j():
        for d in range(1, 8):
            j_take(d).wait_recv()
        row8 = lax.broadcasted_iota(jnp.int32, (8, HD), 0)
        rows = []
        for j in range(4):
            r = tab[SOURCE + j]
            block = jnp.where(row8 % 4 == (r & 3), j_buf[lax.shift_right_logical(r, 2)], 0.0)
            pair = [jnp.sum(block[4 * n : 4 * n + 4], axis=0, keepdims=True) for n in range(2)]
            rows.append(jnp.concatenate(pair, axis=1))
        attended[...] = jnp.concatenate(rows, axis=0).astype(BF16)

    stage_a()
    loads[0].wait()
    for p in range(PIECES):
        migrate(0, p, True)

    on_stage[...] = own[tab[ONCHIP]]
    on_copy = remote(on_stage, onchip, on_sem.at[0], on_sem.at[1], partner)
    on_copy.start()

    migrate(1, 0, False)
    picked = stage_b()
    migrate(1, 1, False)
    migrate(1, 2, False)
    migrate(1, 3, False)
    migrate(2, 0, False)
    wait_b()
    for p in range(4):
        stage_c((2 * p, 2 * p + 1))
        if p < 3:
            migrate(2, p + 1, False)
    send_d()
    migrate(3, 0, False)
    migrate(3, 1, False)
    migrate(3, 2, False)
    stage_d()
    migrate(3, 3, False)
    migrate(4, 0, False)
    migrate(4, 1, False)
    low, high = stage_e(picked)
    loads[1].wait()
    stage_f(low, high, 0, 8)
    migrate(4, 2, False)
    stage_f(low, high, 8, 16)
    send_h()
    migrate(4, 3, False)
    migrate(5, 0, False)
    migrate(5, 1, False)
    migrate(5, 2, False)
    stage_h()
    migrate(5, 3, False)

    def more(s, carry):
        for p in range(PIECES):
            migrate(s, p, False)
        return carry

    if steps > 6:
        for p in range(PIECES):
            migrate(6, p, False)
            if p == 2:
                stage_i()
        if steps > 7:
            lax.fori_loop(7, steps, more, 0)
    end_piece(0)
    end_piece(1)
    if steps == 6:
        stage_i()
    end_piece(2)
    end_piece(3)
    stage_j()

    for p in range(PIECES):
        shares[p].wait_send()
    on_copy.wait()
    for d in range(1, 16):
        a_copy(d).wait_send()
        xy_copy(b_send, b_buf, b_ss, b_rs, d, True).wait_send()
        xy_copy(d_send, d_buf, d_ss, d_rs, d, False).wait_send()
        xy_copy(h_send, h_buf, h_ss, h_rs, d, False).wait_send()
    e_copy().wait_send()
    i_copy().wait_send()
    for d in range(1, 8):
        j_copy(d).wait_send()

    def drain(s, carry):
        for d in range(2):

            @pl.when(has_out(d))
            def _():
                for p in range(PIECES):
                    hop(d, s, p).wait_send()

        return carry

    lax.fori_loop(0, steps, drain, 0)

    def drain_mirror(s, carry):
        for d in range(2):

            @pl.when(has_in(d))
            def _():
                there, here = mirror(d, s, 0, PIECES)
                there.wait()
                here.wait()

        return carry

    lax.fori_loop(0, steps - 1, drain_mirror, 0)
    for d in range(2):

        @pl.when(has_in(d))
        def _():
            for p in range(PIECES):
                there, here = mirror(d, steps - 1, p, 1)
                there.wait()
                here.wait()


def place_kernel(tab, cache, arrived, onchip, out, sems):
    for j in range(4):
        code = tab[PLACE + j]

        @pl.when(code < 4)
        def _():
            pltpu.make_async_copy(cache.at[jnp.minimum(code, 3)], out.at[j], sems.at[j]).start()

        @pl.when(code == 4)
        def _():
            pltpu.make_async_copy(onchip, out.at[j], sems.at[j]).start()

        @pl.when(code > 4)
        def _():
            at = jnp.maximum(code - 8, 0)
            step = jnp.minimum(at & 15, arrived.shape[1] - 1)
            src = arrived.at[lax.shift_right_logical(at, 4), step]
            pltpu.make_async_copy(src, out.at[j], sems.at[j]).start()

    for j in range(4):
        pltpu.make_async_copy(onchip, out.at[j], sems.at[j]).wait()


def variant(number, tab, queries, new_kv, kv_cache, o_weight):
    steps = STEPS[number]
    sem = pltpu.SemaphoreType.DMA
    vmem = pltpu.VMEM
    anywhere = pl.BlockSpec(memory_space=pl.ANY)
    smem = pl.BlockSpec(memory_space=pltpu.SMEM)
    whole = pl.BlockSpec(memory_space=pltpu.VMEM)
    request = kv_cache.shape[1:]
    attended, arrived, onchip = pl.pallas_call(
        functools.partial(main_kernel, steps),
        out_shape=(
            jax.ShapeDtypeStruct((4, 256), BF16),
            jax.ShapeDtypeStruct((2, steps) + request, BF16),
            jax.ShapeDtypeStruct(request, BF16),
        ),
        in_specs=[smem, whole, whole, anywhere, anywhere],
        out_specs=(whole, anywhere, anywhere),
        scratch_shapes=[
            vmem((4, 128, 2048), BF16),
            [vmem((4, ROWS, 2048), BF16) for _ in range(PIECES)],
            vmem((2, steps, 64, 2048), BF16),
            vmem((2, steps, 64, 2048), BF16),
            vmem((128, 2048), BF16),
            vmem((256, 8192), BF16),
            vmem((16, HD), BF16), vmem((16, 16, HD), BF16),
            vmem((16, HD), BF16), vmem((16, 16, HD), BF16),
            vmem((16, 16, 2 * HD), F32), vmem((16, 16, 2 * HD), F32),
            vmem((16, 2 * HD), F32), vmem((16, 2 * HD), F32),
            vmem((16, 8, 256), F32), vmem((16, 8, 256), F32),
            vmem((8, 256), F32), vmem((8, 256), F32),
            vmem((8, HD), F32), vmem((8, 8, HD), F32),
            sem((2, steps, PIECES)), sem((2, steps, PIECES)),
            sem((2, steps, PIECES)), sem((2, steps, PIECES)), sem((2, steps, PIECES)),
            sem((PIECES,)), sem((PIECES,)), sem((2,)), sem((2,)),
            sem((15,)), sem((15,)), sem((15,)), sem((15,)), sem((15,)), sem((15,)),
            sem((2,)), sem((15,)), sem((15,)), sem((2,)), sem((7,)), sem((7,)),
        ],
        compiler_params=pltpu.CompilerParams(
            collective_id=number, has_side_effects=True, vmem_limit_bytes=48 * 2**20
        ),
        name="migrate_and_attend",
    )(tab, queries, new_kv, kv_cache, o_weight)
    new_cache = pl.pallas_call(
        place_kernel,
        out_shape=jax.ShapeDtypeStruct(kv_cache.shape, BF16),
        in_specs=[smem, anywhere, anywhere, anywhere],
        out_specs=anywhere,
        scratch_shapes=[sem((4,))],
        name="place",
    )(tab, kv_cache, arrived, onchip)
    return attended, new_cache


def on_device(queries, new_kv, kv_cache, lengths, move_from, o_weight):
    smem = pl.BlockSpec(memory_space=pltpu.SMEM)
    words = functools.partial(pltpu.SMEM, dtype=jnp.int32)
    tab, pick = pl.pallas_call(
        plan_kernel,
        out_shape=(jax.ShapeDtypeStruct((64,), jnp.int32), jax.ShapeDtypeStruct((1,), jnp.int32)),
        in_specs=[smem, smem],
        out_specs=(smem, smem),
        scratch_shapes=[words((32,)), words((16,)), words((32,)), words((16,)), words((32,))],
        name="plan",
    )(move_from, lengths)
    branches = [functools.partial(variant, n) for n in range(len(STEPS))]
    return lax.switch(pick[0], branches, tab, queries, new_kv, kv_cache, o_weight)


def solution(mesh):
    in_specs = (P("inst", "tp"), P("inst", None), P("inst", "tp", None), P(), P(), P("tp", None))
    out_specs = (P("inst", "tp"), P("inst", "tp", None))
    return jax.shard_map(
        on_device, mesh=mesh, in_specs=in_specs, out_specs=out_specs, check_vma=False
    )
```

```python
import functools

import jax
import jax.numpy as jnp
from jax import lax
from jax.experimental import pallas as pl
from jax.experimental.pallas import tpu as pltpu
from jax.sharding import PartitionSpec as P

MESH = pl.DeviceIdType.MESH
KVH = 8
HD = 128
SCALE = HD ** -0.5
STEPS = (6, 7, 8, 9, 12)
PIECES = 4
ROWS = 16
F32 = jnp.float32
BF16 = jnp.bfloat16

BEGIN, FIRST, LAST, MERGE, PROJECT, SPREAD = (1, 2), (2, 1), (2, 2), (3, 3), (5, 1), (6, 2)

SEND, PLACE, SLOT_OF, LENGTH, SOURCE, ONCHIP, DUMP = 0, 32, 40, 44, 48, 52, 63


def plan_kernel(move_ref, len_ref, tab_ref, pick_ref, slot_of, count, rank, par, free):
    inst = lax.axis_index("inst")
    chip = inst // 2
    tab_ref[ONCHIP] = 0
    for n in range(32):
        tab_ref[SEND + n] = -1
        slot_of[move_ref[n]] = n
    for n in range(16):
        count[n] = 0
    for r in range(32):
        kind = (r // 8) * 4 + lax.shift_right_logical(slot_of[r], 3)
        seen = count[kind]
        rank[r] = seen
        count[kind] = seen + 1
    most = jnp.int32(STEPS[0])
    for d in range(2):

        def number(a, b):
            return count[a * 4 + b] if d == 0 else count[(3 - a) * 4 + 3 - b]

        n02, n03, n12, n13 = number(0, 2), number(0, 3), number(1, 2), number(1, 3)
        o0, o1 = n02 + n03, n12 + n13
        par[d * 8 + 0] = n03
        par[d * 8 + 1] = o0
        par[d * 8 + 2] = n13
        one = jnp.int32(1)
        mask = lax.shift_left(lax.shift_left(one, n03) - 1, jnp.int32(2))
        again = lax.shift_left(lax.shift_left(one, jnp.maximum(n13 - 1, 0)) - 1, o0 + 2)
        mask = mask | jnp.where(n13 > 0, again | 2, 0)
        seen = jnp.int32(0)
        for s in range(10):
            free[d * 16 + seen] = s
            seen = seen + 1 - (lax.shift_right_logical(mask, jnp.int32(s)) & 1)
        most = jnp.maximum(most, o0 + jnp.maximum(o1, jnp.minimum(o0, 1)))
        most = jnp.maximum(most, jnp.where(n13 > 1, o0 + n13 + 1, 0))
    pick = jnp.int32(0)
    for steps in STEPS[:-1]:
        pick = pick + (most > steps).astype(jnp.int32)
    pick_ref[0] = pick

    def first_step(r, a_chip, b_chip):
        d = (b_chip < a_chip).astype(jnp.int32)
        a = jnp.where(d == 1, 3 - a_chip, a_chip)
        b = jnp.where(d == 1, 3 - b_chip, b_chip)
        k = rank[r]
        n03, o0, n13 = par[d * 8], par[d * 8 + 1], par[d * 8 + 2]
        p0 = k + jnp.where(b == 3, 0, jnp.where(b == 2, n03, o0))
        q = jnp.where(b == 3, k, n13 + k)
        p1 = jnp.where(q == 0, 0, o0 + q)
        p2 = free[d * 16 + k]
        return d, jnp.where(a == 0, p0, jnp.where(a == 1, p1, p2)), b - a

    for q in range(8):
        r = chip * 8 + q
        b = lax.shift_right_logical(slot_of[r], 3)
        d, step, _ = first_step(r, chip, b)
        tab_ref[jnp.where(b == chip, DUMP, SEND + d * 16 + step)] = q
    for k in range(4):
        r = inst * 4 + k
        g = slot_of[r]
        home = lax.shift_right_logical(g, 2)
        tab_ref[jnp.where((home != inst) & (home // 2 == chip), ONCHIP, DUMP)] = k
        tab_ref[SLOT_OF + k] = g
        tab_ref[LENGTH + k] = len_ref[r]
    for j in range(4):
        r = move_ref[inst * 4 + j]
        home = lax.shift_right_logical(r, 2)
        a = lax.shift_right_logical(r, 3)
        d, step, hops = first_step(r, a, chip)
        arrival = 8 + d * 16 + step + hops - 1
        tab_ref[PLACE + j] = jnp.where(home == inst, r & 3, jnp.where(a == chip, 4, arrival))
        tab_ref[SOURCE + j] = r


def main_kernel(
    steps, tab, q_ref, new_ref, cache, weight, attended, new_cache,
    own, part, tx, rx, on_stage, on_buf, placed, w_buf,
    a_send, a_buf, b_send, b_buf, d_send, d_buf, e_send, e_buf, h_send, h_buf, j_send, j_buf,
    tx_sem, rx_sem, mir_send, mir_recv, part_send, part_recv, on_sem, load_sem, out_sem,
    a_ss, a_rs, b_ss, b_rs, d_ss, d_rs, e_sem, h_ss, h_rs, j_ss, j_rs,
):
    inst = lax.axis_index("inst")
    tp = lax.axis_index("tp")
    chip, core = inst // 2, inst % 2
    zh, u = tp % 2, tp // 2
    me = zh * 8 + inst
    partner = {"inst": chip * 2 + 1 - core}
    z_partner = {"tp": u * 2 + 1 - zh}

    def peer16(d):
        e = (me + d) % 16
        return {"inst": e % 8, "tp": u * 2 + e // 8}

    def peer_xy(d):
        return {"tp": ((u + d) % 16) * 2 + zh}

    def remote(src, dst, ss, rs, to):
        return pltpu.make_async_remote_copy(
            src_ref=src, dst_ref=dst, send_sem=ss, recv_sem=rs, device_id=to, device_id_type=MESH
        )

    half = pl.multiple_of(core * 64, 64)
    other = pl.multiple_of(64 - core * 64, 64)
    loads = [
        pltpu.make_async_copy(cache, own, load_sem.at[0]),
        pltpu.make_async_copy(weight, w_buf, load_sem.at[1]),
    ]
    for load in loads:
        load.start()

    lanes = pl.ds(pl.multiple_of((u // 2) * HD, HD), HD)
    value_lanes = pl.ds(pl.multiple_of(KVH * HD + (u // 2) * HD, HD), HD)
    q = q_ref[...].astype(F32)
    packed = jnp.concatenate(
        [q[:, :HD], q[:, HD:], new_ref[:, lanes].astype(F32), new_ref[:, value_lanes].astype(F32)], axis=0
    ).astype(BF16)
    a_send[...] = packed
    a_buf[pl.ds(me, 1)] = packed[None]

    barrier = pltpu.get_barrier_semaphore()
    for d in range(1, 16):
        pl.semaphore_signal(barrier, inc=1, device_id=peer16(d), device_id_type=MESH)
        pl.semaphore_signal(barrier, inc=1, device_id=peer_xy(d), device_id_type=MESH)
    pl.semaphore_wait(barrier, 30)

    def a_copy(d):
        return remote(a_send, a_buf.at[me], a_ss.at[d - 1], a_rs.at[d - 1], peer16(d))

    def a_take(d):
        return remote(a_send, a_buf.at[(me + 16 - d) % 16], a_ss.at[d - 1], a_rs.at[d - 1], peer16(d))

    shares = [
        remote(
            cache.at[:, pl.ds(pl.multiple_of(other + p * ROWS, ROWS), ROWS)],
            part[p], part_send.at[p], part_recv.at[p], partner,
        )
        for p in range(PIECES)
    ]
    shares[0].start()
    for d in range(1, 16):
        a_copy(d).start()
    for share in shares[1:]:
        share.start()

    def has_in(d):
        return chip > 0 if d == 0 else chip < 3

    def has_out(d):
        return chip < 3 if d == 0 else chip > 0

    def hop(d, s, p):
        to = {"inst": jnp.clip(inst + (2 if d == 0 else -2), 0, 7)}
        src = tx.at[d, s, pl.ds(p * ROWS, ROWS)]
        dst = rx.at[d, s, pl.ds(pl.multiple_of(half + p * ROWS, ROWS), ROWS)]
        return remote(src, dst, tx_sem.at[d, s, p], rx_sem.at[d, s, p], to)

    def mirror(d, s, p0, count):
        block = rx.at[d, s, pl.ds(pl.multiple_of(half + p0 * ROWS, ROWS), count * ROWS)]
        return remote(block, block, mir_send.at[d, s, p0], mir_recv.at[d, s, p0], partner)

    def migrate(s, p, first, old=False):
        rows = pl.ds(p * ROWS, ROWS)
        if first:
            shares[p].wait_recv()
        own_rows = pl.ds(pl.multiple_of(half + p * ROWS, ROWS), ROWS)
        for d in range(2):
            if not first:

                @pl.when(has_in(d))
                def _():
                    hop(d, s - 1, p).wait_recv()

            @pl.when(has_out(d))
            def _():
                code = tab[SEND + d * 16 + s]
                choice = jnp.maximum(code, 0)
                mine = lax.shift_right_logical(choice, 2) == core
                index = choice & 3
                block = jnp.where(mine, own[index, own_rows, :], part[p][index])
                if not first:
                    block = jnp.where(code < 0, rx[d, s - 1, own_rows, :], block)
                tx[d, s, rows, :] = block
                hop(d, s, p).start()
                if old:
                    hop(d, s - 2, p).wait_send()

            if not first and p == PIECES - 1:

                @pl.when(has_in(d))
                def _():
                    mirror(d, s - 1, 0, PIECES).start()
                    if old:
                        mirror(d, s - 2, 0, PIECES).wait()

    def end_piece(p):
        for d in range(2):

            @pl.when(has_in(d))
            def _():
                hop(d, steps - 1, p).wait_recv()
                mirror(d, steps - 1, p, 1).start()

    row16 = lax.broadcasted_iota(jnp.int32, (16, 1), 0)

    def by_slot(kind, values):
        out = jnp.full(kind.shape, values[0], jnp.int32)
        for k in range(1, 4):
            out = jnp.where(kind == k, values[k], out)
        return out

    def xy_copy(send, buf, ss, rs, d, whole):
        src = send if whole else send.at[(u + d) % 16]
        return remote(src, buf.at[u], ss.at[d - 1], rs.at[d - 1], peer_xy(d))

    def xy_take(send, buf, ss, rs, d, whole):
        src = send if whole else send.at[(u + d) % 16]
        return remote(src, buf.at[(u + 16 - d) % 16], ss.at[d - 1], rs.at[d - 1], peer_xy(d))

    def stage_b():
        for d in range(1, 16):
            a_take(d).wait_recv()
        blocks, spots = [], []
        for k in range(4):
            g = tab[SLOT_OF + k]
            spots.append(g & 3)
            for z in range(2):
                blocks.append(a_buf[z * 8 + lax.shift_right_logical(g, 2)])
        stacked = jnp.concatenate(blocks, axis=0)
        row = lax.broadcasted_iota(jnp.int32, (48, 128), 0)
        col = lax.broadcasted_iota(jnp.int32, (48, 128), 1)
        inner = row % 16
        k, h, group = inner // 4, inner % 4, row // 16
        spot = by_slot(k, spots)
        place = jnp.where(
            group == 0, (k * 2 + h // 2) * 16 + (h % 2) * 4, k * 32 + 4 + group * 4
        )
        chosen = (col == place + spot).astype(F32).astype(BF16)
        picked = jnp.dot(chosen, stacked, preferred_element_type=F32)
        mine = picked[:16].astype(BF16)
        b_send[...] = mine
        b_buf[pl.ds(u, 1)] = mine[None]
        for d in range(1, 16):
            xy_copy(b_send, b_buf, b_ss, b_rs, d, True).start()
        return picked

    def wait_b():
        for d in range(1, 16):
            xy_take(b_send, b_buf, b_ss, b_rs, d, True).wait_recv()

    row32 = lax.broadcasted_iota(jnp.int32, (32, 1), 0)
    of_row = (row32 % 16) // 4

    def stage_c(heads):
        limit = by_slot(of_row, [tab[LENGTH + k] for k in range(4)])
        position = tp * 128 + lax.broadcasted_iota(jnp.int32, (32, 128), 1)
        usable = position < limit
        for k in heads:
            query = b_buf[2 * k : 2 * k + 2].reshape(32, HD)
            keys = own[:, :, k * HD : (k + 1) * HD].reshape(512, HD)
            values = own[:, :, (KVH + k) * HD : (KVH + k + 1) * HD].reshape(512, HD)
            full = lax.dot_general(query, keys, (((1,), (1,)), ((), ())), preferred_element_type=F32)
            scores = full[:, :128]
            for r in range(1, 4):
                scores = jnp.where(of_row == r, full[:, r * 128 : (r + 1) * 128], scores)
            masked = jnp.where(usable, scores * SCALE, -1e30)
            top = jnp.max(masked, axis=1, keepdims=True)
            weights = jnp.where(usable, jnp.exp(masked - top), 0.0)
            total = jnp.sum(weights, axis=1, keepdims=True)
            spread = jnp.concatenate(
                [jnp.where(of_row == r, weights, 0.0).astype(BF16) for r in range(4)], axis=1
            )
            summed = jnp.dot(spread, values, preferred_element_type=F32)
            lane = lax.broadcasted_iota(jnp.int32, (32, HD), 1)
            stats = jnp.where(lane < 64, top, total)
            d_send[2 * k : 2 * k + 2] = jnp.concatenate([summed, stats], axis=1).reshape(2, 16, 2 * HD)
            for to in (2 * k, 2 * k + 1):

                @pl.when(u != to)
                def _():
                    d_copy(to).start()

                @pl.when(u == to)
                def _():
                    d_buf[to] = d_send[to]

    def d_copy(to):
        there = {"tp": to * 2 + zh}
        return remote(d_send.at[to], d_buf.at[u], d_ss.at[to], d_rs.at[u], there)

    def d_take(n):
        there = {"tp": n * 2 + zh}
        return remote(d_send.at[n], d_buf.at[n], d_ss.at[n], d_rs.at[n], there)

    def merge(blocks):
        tops = [block[:, HD : HD + 1] for block in blocks]
        top = functools.reduce(jnp.maximum, tops)
        factors = [jnp.exp(t - top) for t in tops]
        summed = sum(block[:, :HD] * f for block, f in zip(blocks, factors))
        total = sum(block[:, HD + 64 : HD + 65] * f for block, f in zip(blocks, factors))
        return top, total, summed

    def e_copy():
        return remote(e_send, e_buf, e_sem.at[0], e_sem.at[1], z_partner)

    def stage_d():
        for n in range(16):

            @pl.when(u != n)
            def _():
                d_take(n).wait_recv()

        top, total, summed = merge([d_buf[n] for n in range(16)])
        lane = lax.broadcasted_iota(jnp.int32, (16, HD), 1)
        e_send[...] = jnp.concatenate([summed, jnp.where(lane < 64, top, total)], axis=1)
        e_copy().start()

    def stage_e(picked):
        e_copy().wait_recv()
        top, total, summed = merge([e_send[...], e_buf[...]])
        query, key, value = picked[:16], picked[16:32], picked[32:48]
        own_score = jnp.sum(query * key, axis=1, keepdims=True) * SCALE
        highest = jnp.maximum(top, own_score)
        old, new = jnp.exp(top - highest), jnp.exp(own_score - highest)
        attention = ((summed * old + new * value) / (total * old + new)).astype(BF16)
        row = lax.broadcasted_iota(jnp.int32, (16, 16), 0)
        col = lax.broadcasted_iota(jnp.int32, (16, 16), 1)
        heads = []
        for h in range(2):
            chosen = ((col == (row % 4) * 4 + zh * 2 + h) & (row < 8)).astype(F32).astype(BF16)
            heads.append(jnp.dot(chosen, attention, preferred_element_type=F32))
        both = jnp.concatenate(heads, axis=1)
        low = jnp.where(row16 < 4, both, 0.0).astype(BF16)
        high = jnp.where(row16 >= 4, both, 0.0).astype(BF16)
        return low, high

    def stage_f(low, high, first, last):
        for n in range(first, last):
            at = n * 512
            out = jnp.dot(low, w_buf[:, at : at + 256], preferred_element_type=F32)
            out = out + jnp.dot(high, w_buf[:, at + 256 : at + 512], preferred_element_type=F32)
            h_send[n] = out[:8]

    def send_h():
        h_buf[pl.ds(u, 1)] = h_send[pl.ds(u, 1)]
        for d in range(1, 16):
            xy_copy(h_send, h_buf, h_ss, h_rs, d, False).start()

    def j_copy(d):
        return remote(j_send, j_buf.at[me], j_ss.at[d - 1], j_rs.at[d - 1], peer16(d))

    def j_take(d):
        return remote(j_send, j_buf.at[(me + 16 - d) % 16], j_ss.at[d - 1], j_rs.at[d - 1], peer16(d))

    def stage_h():
        for d in range(1, 16):
            xy_take(h_send, h_buf, h_ss, h_rs, d, False).wait_recv()
        total = sum(h_buf[n] for n in range(16))
        j_send[...] = total
        j_buf[pl.ds(me, 1)] = total[None]
        for d in range(1, 16):
            j_copy(d).start()

    def stage_j():
        for d in range(1, 16):
            j_take(d).wait_recv()
        row8 = lax.broadcasted_iota(jnp.int32, (8, 256), 0)
        rows = []
        for j in range(4):
            r = tab[SOURCE + j]
            home = lax.shift_right_logical(r, 2)
            block = j_buf[home] + j_buf[8 + home]
            block = jnp.where(row8 == zh * 4 + (r & 3), block, 0.0)
            rows.append(jnp.sum(block, axis=0, keepdims=True))
        attended[...] = jnp.concatenate(rows, axis=0).astype(BF16)

    def place(j):
        code = tab[PLACE + j]
        mine = jnp.minimum(code, 3)
        at = jnp.maximum(code - 8, 0)
        side, step = lax.shift_right_logical(at, 4), jnp.minimum(at & 15, steps - 1)

        def block(n, carry):
            rows = pl.ds(pl.multiple_of(n * ROWS, ROWS), ROWS)
            near = jnp.where(code < 4, own[mine, rows, :], on_buf[rows, :])
            placed[j, rows, :] = jnp.where(code < 5, near, rx[side, step, rows, :])
            return carry

        lax.fori_loop(0, 128 // ROWS, block, 0)
        pltpu.make_async_copy(placed.at[j], new_cache.at[j], out_sem.at[j]).start()

    loads[0].wait()
    for p in range(PIECES):
        migrate(0, p, True)

    on_stage[...] = own[tab[ONCHIP]]
    on_copy = remote(on_stage, on_buf, on_sem.at[0], on_sem.at[1], partner)
    on_copy.start()

    kept = {}

    def after_e():
        low, high = stage_e(kept["picked"])
        loads[1].wait()
        stage_f(low, high, 0, 16)
        send_h()

    def begin():
        kept["picked"] = stage_b()

    def first_heads():
        wait_b()
        stage_c(range(0, 4))

    def last_heads():
        stage_c(range(4, 8))

    timetable = {BEGIN: begin, FIRST: first_heads, LAST: last_heads, MERGE: stage_d, PROJECT: after_e, SPREAD: stage_h}
    for s in range(1, min(steps, 7)):
        for p in range(PIECES):
            migrate(s, p, False, old=s >= 2)
            if (s, p) in timetable:
                timetable[s, p]()

    def more(s, carry):
        for p in range(PIECES):
            migrate(s, p, False, old=True)
        return carry

    if steps > 7:
        lax.fori_loop(7, steps, more, 0)
    for p in range(PIECES):
        end_piece(p)
        if (steps, p) in timetable and steps == 6:
            timetable[steps, p]()

    on_copy.wait()
    for d in range(2):

        @pl.when(has_in(d))
        def _():
            mirror(d, steps - 2, 0, PIECES).wait()
            for p in range(PIECES):
                mirror(d, steps - 1, p, 1).wait()

    for j in range(4):
        place(j)
    stage_j()

    for p in range(PIECES):
        shares[p].wait_send()
    for d in range(1, 16):
        a_copy(d).wait_send()
        xy_copy(b_send, b_buf, b_ss, b_rs, d, True).wait_send()
        xy_copy(h_send, h_buf, h_ss, h_rs, d, False).wait_send()
        j_copy(d).wait_send()
    for n in range(16):

        @pl.when(u != n)
        def _():
            d_copy(n).wait_send()

    e_copy().wait_send()
    for d in range(2):

        @pl.when(has_out(d))
        def _():
            for s in (steps - 2, steps - 1):
                for p in range(PIECES):
                    hop(d, s, p).wait_send()

    for j in range(4):
        pltpu.make_async_copy(placed.at[j], new_cache.at[j], out_sem.at[j]).wait()


def variant(number, tab, queries, new_kv, kv_cache, o_weight):
    steps = STEPS[number]
    sem = pltpu.SemaphoreType.DMA
    vmem = pltpu.VMEM
    anywhere = pl.BlockSpec(memory_space=pl.ANY)
    smem = pl.BlockSpec(memory_space=pltpu.SMEM)
    whole = pl.BlockSpec(memory_space=pltpu.VMEM)
    return pl.pallas_call(
        functools.partial(main_kernel, steps),
        out_shape=(jax.ShapeDtypeStruct((4, 256), BF16), jax.ShapeDtypeStruct(kv_cache.shape, BF16)),
        in_specs=[smem, whole, whole, anywhere, anywhere],
        out_specs=(whole, anywhere),
        scratch_shapes=[
            vmem((4, 128, 2048), BF16),
            [vmem((4, ROWS, 2048), BF16) for _ in range(PIECES)],
            vmem((2, steps, 64, 2048), BF16),
            vmem((2, steps, 128, 2048), BF16),
            vmem((128, 2048), BF16), vmem((128, 2048), BF16),
            vmem((4, 128, 2048), BF16),
            vmem((256, 8192), BF16),
            vmem((16, HD), BF16), vmem((16, 16, HD), BF16),
            vmem((16, HD), BF16), vmem((16, 16, HD), BF16),
            vmem((16, 16, 2 * HD), F32), vmem((16, 16, 2 * HD), F32),
            vmem((16, 2 * HD), F32), vmem((16, 2 * HD), F32),
            vmem((16, 8, 256), F32), vmem((16, 8, 256), F32),
            vmem((8, 256), F32), vmem((16, 8, 256), F32),
            sem((2, steps, PIECES)), sem((2, steps, PIECES)),
            sem((2, steps, PIECES)), sem((2, steps, PIECES)),
            sem((PIECES,)), sem((PIECES,)), sem((2,)), sem((2,)), sem((4,)),
            sem((15,)), sem((15,)), sem((15,)), sem((15,)), sem((16,)), sem((16,)),
            sem((2,)), sem((15,)), sem((15,)), sem((15,)), sem((15,)),
        ],
        compiler_params=pltpu.CompilerParams(
            collective_id=number, has_side_effects=True, vmem_limit_bytes=56 * 2**20
        ),
        name="migrate_and_attend",
    )(tab, queries, new_kv, kv_cache, o_weight)


def on_device(queries, new_kv, kv_cache, lengths, move_from, o_weight):
    smem = pl.BlockSpec(memory_space=pltpu.SMEM)
    words = functools.partial(pltpu.SMEM, dtype=jnp.int32)
    tab, pick = pl.pallas_call(
        plan_kernel,
        out_shape=(jax.ShapeDtypeStruct((64,), jnp.int32), jax.ShapeDtypeStruct((1,), jnp.int32)),
        in_specs=[smem, smem],
        out_specs=(smem, smem),
        scratch_shapes=[words((32,)), words((16,)), words((32,)), words((16,)), words((32,))],
        name="plan",
    )(move_from, lengths)
    branches = [functools.partial(variant, n) for n in range(len(STEPS))]
    return lax.switch(pick[0], branches, tab, queries, new_kv, kv_cache, o_weight)


def solution(mesh):
    in_specs = (P("inst", "tp"), P("inst", None), P("inst", "tp", None), P(), P(), P("tp", None))
    out_specs = (P("inst", "tp"), P("inst", "tp", None))
    return jax.shard_map(
        on_device, mesh=mesh, in_specs=in_specs, out_specs=out_specs, check_vma=False
    )
```

```python
import functools

import jax
import jax.numpy as jnp
from jax import lax
from jax.experimental import pallas as pl
from jax.experimental.pallas import tpu as pltpu
from jax.sharding import PartitionSpec as P

MESH = pl.DeviceIdType.MESH
KVH = 8
HD = 128
SCALE = HD ** -0.5
STEPS = (6, 7, 8, 9, 12)
PIECES = 4
ROWS = 16
F32 = jnp.float32
BF16 = jnp.bfloat16

BEGIN, FIRST, LAST, MERGE, PROJECT, SPREAD = (1, 2), (2, 1), (2, 2), (3, 3), (5, 1), (6, 2)

SEND, PLACE, SLOT_OF, LENGTH, SOURCE, ONCHIP, DUMP = 0, 32, 40, 44, 48, 52, 63


def plan_kernel(move_ref, len_ref, tab_ref, pick_ref, slot_of, count, rank, par, free):
    inst = lax.axis_index("inst")
    chip = inst // 2
    tab_ref[ONCHIP] = 0
    for n in range(32):
        tab_ref[SEND + n] = -1
        slot_of[move_ref[n]] = n
    for n in range(16):
        count[n] = 0
    for r in range(32):
        kind = (r // 8) * 4 + lax.shift_right_logical(slot_of[r], 3)
        seen = count[kind]
        rank[r] = seen
        count[kind] = seen + 1
    most = jnp.int32(STEPS[0])
    for d in range(2):

        def number(a, b):
            return count[a * 4 + b] if d == 0 else count[(3 - a) * 4 + 3 - b]

        n02, n03, n12, n13 = number(0, 2), number(0, 3), number(1, 2), number(1, 3)
        o0, o1 = n02 + n03, n12 + n13
        par[d * 8 + 0] = n03
        par[d * 8 + 1] = o0
        par[d * 8 + 2] = n13
        one = jnp.int32(1)
        mask = lax.shift_left(lax.shift_left(one, n03) - 1, jnp.int32(2))
        again = lax.shift_left(lax.shift_left(one, jnp.maximum(n13 - 1, 0)) - 1, o0 + 2)
        mask = mask | jnp.where(n13 > 0, again | 2, 0)
        seen = jnp.int32(0)
        for s in range(10):
            free[d * 16 + seen] = s
            seen = seen + 1 - (lax.shift_right_logical(mask, jnp.int32(s)) & 1)
        most = jnp.maximum(most, o0 + jnp.maximum(o1, jnp.minimum(o0, 1)))
        most = jnp.maximum(most, jnp.where(n13 > 1, o0 + n13 + 1, 0))
    pick = jnp.int32(0)
    for steps in STEPS[:-1]:
        pick = pick + (most > steps).astype(jnp.int32)
    pick_ref[0] = pick

    def first_step(r, a_chip, b_chip):
        d = (b_chip < a_chip).astype(jnp.int32)
        a = jnp.where(d == 1, 3 - a_chip, a_chip)
        b = jnp.where(d == 1, 3 - b_chip, b_chip)
        k = rank[r]
        n03, o0, n13 = par[d * 8], par[d * 8 + 1], par[d * 8 + 2]
        p0 = k + jnp.where(b == 3, 0, jnp.where(b == 2, n03, o0))
        q = jnp.where(b == 3, k, n13 + k)
        p1 = jnp.where(q == 0, 0, o0 + q)
        p2 = free[d * 16 + k]
        return d, jnp.where(a == 0, p0, jnp.where(a == 1, p1, p2)), b - a

    for q in range(8):
        r = chip * 8 + q
        b = lax.shift_right_logical(slot_of[r], 3)
        d, step, _ = first_step(r, chip, b)
        tab_ref[jnp.where(b == chip, DUMP, SEND + d * 16 + step)] = q
    for k in range(4):
        r = inst * 4 + k
        g = slot_of[r]
        home = lax.shift_right_logical(g, 2)
        tab_ref[jnp.where((home != inst) & (home // 2 == chip), ONCHIP, DUMP)] = k
        tab_ref[SLOT_OF + k] = g
        tab_ref[LENGTH + k] = len_ref[r]
    for j in range(4):
        r = move_ref[inst * 4 + j]
        home = lax.shift_right_logical(r, 2)
        a = lax.shift_right_logical(r, 3)
        d, step, hops = first_step(r, a, chip)
        arrival = 8 + d * 16 + step + hops - 1
        tab_ref[PLACE + j] = jnp.where(home == inst, r & 3, jnp.where(a == chip, 4, arrival))
        tab_ref[SOURCE + j] = r


def main_kernel(
    steps, tab, q_ref, new_ref, cache, weight, attended, new_cache,
    own, part, tx, rx, on_stage, on_buf, placed, w_buf,
    a_send, a_buf, b_send, b_buf, d_send, d_buf, e_send, e_buf, h_send, h_buf, j_send, j_buf,
    tx_sem, rx_sem, mir_send, mir_recv, part_send, part_recv, on_sem, load_sem, out_sem,
    a_ss, a_rs, b_ss, b_rs, d_ss, d_rs, e_sem, h_ss, h_rs, j_ss, j_rs,
):
    inst = lax.axis_index("inst")
    tp = lax.axis_index("tp")
    chip, core = inst // 2, inst % 2
    zh, u = tp % 2, tp // 2
    me = zh * 8 + inst
    partner = {"inst": chip * 2 + 1 - core}
    z_partner = {"tp": u * 2 + 1 - zh}

    def peer16(d):
        e = (me + d) % 16
        return {"inst": e % 8, "tp": u * 2 + e // 8}

    def peer_xy(d):
        return {"tp": ((u + d) % 16) * 2 + zh}

    def remote(src, dst, ss, rs, to):
        return pltpu.make_async_remote_copy(
            src_ref=src, dst_ref=dst, send_sem=ss, recv_sem=rs, device_id=to, device_id_type=MESH
        )

    half = pl.multiple_of(core * 64, 64)
    other = pl.multiple_of(64 - core * 64, 64)
    loads = [
        pltpu.make_async_copy(cache, own, load_sem.at[0]),
        pltpu.make_async_copy(weight, w_buf, load_sem.at[1]),
    ]
    for load in loads:
        load.start()

    lanes = pl.ds(pl.multiple_of((u // 2) * HD, HD), HD)
    value_lanes = pl.ds(pl.multiple_of(KVH * HD + (u // 2) * HD, HD), HD)
    q = q_ref[...].astype(F32)
    packed = jnp.concatenate(
        [q[:, :HD], q[:, HD:], new_ref[:, lanes].astype(F32), new_ref[:, value_lanes].astype(F32)], axis=0
    ).astype(BF16)
    a_send[...] = packed
    a_buf[pl.ds(me, 1)] = packed[None]

    barrier = pltpu.get_barrier_semaphore()
    for d in range(1, 16):
        pl.semaphore_signal(barrier, inc=1, device_id=peer16(d), device_id_type=MESH)
        pl.semaphore_signal(barrier, inc=1, device_id=peer_xy(d), device_id_type=MESH)
    pl.semaphore_wait(barrier, 30)

    def a_copy(d):
        return remote(a_send, a_buf.at[me], a_ss.at[d - 1], a_rs.at[d - 1], peer16(d))

    def a_take(d):
        return remote(a_send, a_buf.at[(me + 16 - d) % 16], a_ss.at[d - 1], a_rs.at[d - 1], peer16(d))

    shares = [
        remote(
            cache.at[:, pl.ds(pl.multiple_of(other + p * ROWS, ROWS), ROWS)],
            part[p], part_send.at[p], part_recv.at[p], partner,
        )
        for p in range(PIECES)
    ]
    shares[0].start()
    for d in range(1, 16):
        a_copy(d).start()
    for share in shares[1:]:
        share.start()

    def has_in(d):
        return chip > 0 if d == 0 else chip < 3

    def has_out(d):
        return chip < 3 if d == 0 else chip > 0

    def hop(d, s, p):
        to = {"inst": jnp.clip(inst + (2 if d == 0 else -2), 0, 7)}
        src = tx.at[d, s, pl.ds(p * ROWS, ROWS)]
        dst = rx.at[d, s, pl.ds(pl.multiple_of(half + p * ROWS, ROWS), ROWS)]
        return remote(src, dst, tx_sem.at[d, s, p], rx_sem.at[d, s, p], to)

    def mirror(d, s, p0, count):
        block = rx.at[d, s, pl.ds(pl.multiple_of(half + p0 * ROWS, ROWS), count * ROWS)]
        return remote(block, block, mir_send.at[d, s, p0], mir_recv.at[d, s, p0], partner)

    def migrate(s, p, first, old=False):
        rows = pl.ds(p * ROWS, ROWS)
        if first:
            shares[p].wait_recv()
        own_rows = pl.ds(pl.multiple_of(half + p * ROWS, ROWS), ROWS)
        for d in range(2):
            if not first:

                @pl.when(has_in(d))
                def _():
                    hop(d, s - 1, p).wait_recv()

            @pl.when(has_out(d))
            def _():
                code = tab[SEND + d * 16 + s]
                choice = jnp.maximum(code, 0)
                mine = lax.shift_right_logical(choice, 2) == core
                index = choice & 3
                block = jnp.where(mine, own[index, own_rows, :], part[p][index])
                if not first:
                    block = jnp.where(code < 0, rx[d, s - 1, own_rows, :], block)
                tx[d, s, rows, :] = block
                hop(d, s, p).start()
                if old:
                    hop(d, s - 2, p).wait_send()

            if not first and p == PIECES - 1:

                @pl.when(has_in(d))
                def _():
                    mirror(d, s - 1, 0, PIECES).start()
                    if old:
                        mirror(d, s - 2, 0, PIECES).wait()

    def end_piece(p):
        for d in range(2):

            @pl.when(has_in(d))
            def _():
                hop(d, steps - 1, p).wait_recv()
                mirror(d, steps - 1, p, 1).start()

    row16 = lax.broadcasted_iota(jnp.int32, (16, 1), 0)

    def by_slot(kind, values):
        out = jnp.full(kind.shape, values[0], jnp.int32)
        for k in range(1, 4):
            out = jnp.where(kind == k, values[k], out)
        return out

    def xy_copy(send, buf, ss, rs, d, whole):
        src = send if whole else send.at[(u + d) % 16]
        return remote(src, buf.at[u], ss.at[d - 1], rs.at[d - 1], peer_xy(d))

    def xy_take(send, buf, ss, rs, d, whole):
        src = send if whole else send.at[(u + d) % 16]
        return remote(src, buf.at[(u + 16 - d) % 16], ss.at[d - 1], rs.at[d - 1], peer_xy(d))

    def stage_b():
        for d in range(1, 16):
            a_take(d).wait_recv()
        blocks, spots = [], []
        for k in range(4):
            g = tab[SLOT_OF + k]
            spots.append(g & 3)
            for z in range(2):
                blocks.append(a_buf[z * 8 + lax.shift_right_logical(g, 2)])
        stacked = jnp.concatenate(blocks, axis=0)
        row = lax.broadcasted_iota(jnp.int32, (48, 128), 0)
        col = lax.broadcasted_iota(jnp.int32, (48, 128), 1)
        inner = row % 16
        k, h, group = inner // 4, inner % 4, row // 16
        spot = by_slot(k, spots)
        place = jnp.where(
            group == 0, (k * 2 + h // 2) * 16 + (h % 2) * 4, k * 32 + 4 + group * 4
        )
        chosen = (col == place + spot).astype(F32).astype(BF16)
        picked = jnp.dot(chosen, stacked, preferred_element_type=F32)
        mine = picked[:16].astype(BF16)
        b_send[...] = mine
        b_buf[pl.ds(u, 1)] = mine[None]
        for d in range(1, 16):
            xy_copy(b_send, b_buf, b_ss, b_rs, d, True).start()
        return picked

    def wait_b():
        for d in range(1, 16):
            xy_take(b_send, b_buf, b_ss, b_rs, d, True).wait_recv()

    row32 = lax.broadcasted_iota(jnp.int32, (32, 1), 0)
    of_row = (row32 % 16) // 4

    def stage_c(heads):
        limit = by_slot(of_row, [tab[LENGTH + k] for k in range(4)])
        position = tp * 128 + lax.broadcasted_iota(jnp.int32, (32, 128), 1)
        usable = position < limit
        for k in heads:
            query = b_buf[2 * k : 2 * k + 2].reshape(32, HD)
            keys = own[:, :, k * HD : (k + 1) * HD].reshape(512, HD)
            values = own[:, :, (KVH + k) * HD : (KVH + k + 1) * HD].reshape(512, HD)
            full = lax.dot_general(query, keys, (((1,), (1,)), ((), ())), preferred_element_type=F32)
            scores = full[:, :128]
            for r in range(1, 4):
                scores = jnp.where(of_row == r, full[:, r * 128 : (r + 1) * 128], scores)
            masked = jnp.where(usable, scores * SCALE, -1e30)
            top = jnp.max(masked, axis=1, keepdims=True)
            weights = jnp.where(usable, jnp.exp(masked - top), 0.0)
            total = jnp.sum(weights, axis=1, keepdims=True)
            spread = jnp.concatenate(
                [jnp.where(of_row == r, weights, 0.0).astype(BF16) for r in range(4)], axis=1
            )
            summed = jnp.dot(spread, values, preferred_element_type=F32)
            lane = lax.broadcasted_iota(jnp.int32, (32, HD), 1)
            stats = jnp.where(lane < 64, top, total)
            d_send[2 * k : 2 * k + 2] = jnp.concatenate([summed, stats], axis=1).reshape(2, 16, 2 * HD)
            for to in (2 * k, 2 * k + 1):

                @pl.when(u != to)
                def _():
                    d_copy(to).start()

                @pl.when(u == to)
                def _():
                    d_buf[to] = d_send[to]

    def d_copy(to):
        there = {"tp": to * 2 + zh}
        return remote(d_send.at[to], d_buf.at[u], d_ss.at[to], d_rs.at[u], there)

    def d_take(n):
        there = {"tp": n * 2 + zh}
        return remote(d_send.at[n], d_buf.at[n], d_ss.at[n], d_rs.at[n], there)

    def merge(blocks):
        tops = [block[:, HD : HD + 1] for block in blocks]
        top = functools.reduce(jnp.maximum, tops)
        factors = [jnp.exp(t - top) for t in tops]
        summed = sum(block[:, :HD] * f for block, f in zip(blocks, factors))
        total = sum(block[:, HD + 64 : HD + 65] * f for block, f in zip(blocks, factors))
        return top, total, summed

    def e_copy():
        return remote(e_send, e_buf, e_sem.at[0], e_sem.at[1], z_partner)

    def stage_d():
        for n in range(16):

            @pl.when(u != n)
            def _():
                d_take(n).wait_recv()

        top, total, summed = merge([d_buf[n] for n in range(16)])
        lane = lax.broadcasted_iota(jnp.int32, (16, HD), 1)
        e_send[...] = jnp.concatenate([summed, jnp.where(lane < 64, top, total)], axis=1)
        e_copy().start()

    def stage_e(picked):
        e_copy().wait_recv()
        top, total, summed = merge([e_send[...], e_buf[...]])
        query, key, value = picked[:16], picked[16:32], picked[32:48]
        own_score = jnp.sum(query * key, axis=1, keepdims=True) * SCALE
        highest = jnp.maximum(top, own_score)
        old, new = jnp.exp(top - highest), jnp.exp(own_score - highest)
        attention = ((summed * old + new * value) / (total * old + new)).astype(BF16)
        row = lax.broadcasted_iota(jnp.int32, (16, 16), 0)
        col = lax.broadcasted_iota(jnp.int32, (16, 16), 1)
        heads = []
        for h in range(2):
            chosen = ((col == (row % 4) * 4 + zh * 2 + h) & (row < 8)).astype(F32).astype(BF16)
            heads.append(jnp.dot(chosen, attention, preferred_element_type=F32))
        both = jnp.concatenate(heads, axis=1)
        low = jnp.where(row16 < 4, both, 0.0).astype(BF16)
        high = jnp.where(row16 >= 4, both, 0.0).astype(BF16)
        return low, high

    def stage_f(low, high, first, last):
        for n in range(first, last):
            at = n * 512
            out = jnp.dot(low, w_buf[:, at : at + 256], preferred_element_type=F32)
            out = out + jnp.dot(high, w_buf[:, at + 256 : at + 512], preferred_element_type=F32)
            h_send[n] = out[:8]

    def send_h():
        h_buf[pl.ds(u, 1)] = h_send[pl.ds(u, 1)]
        for d in range(1, 16):
            xy_copy(h_send, h_buf, h_ss, h_rs, d, False).start()

    def j_copy(d):
        half_of_z = j_send.at[((me + d) % 16) // 8]
        return remote(half_of_z, j_buf.at[me], j_ss.at[d - 1], j_rs.at[d - 1], peer16(d))

    def j_take(d):
        return remote(j_send.at[0], j_buf.at[(me + 16 - d) % 16], j_ss.at[d - 1], j_rs.at[d - 1], peer16(d))

    def stage_h():
        for d in range(1, 16):
            xy_take(h_send, h_buf, h_ss, h_rs, d, False).wait_recv()
        total = sum(h_buf[n] for n in range(16))
        for z in range(2):
            rows = total[4 * z : 4 * z + 4]
            j_send[z] = jnp.concatenate([rows[:, :HD], rows[:, HD:]], axis=0)
        j_buf[pl.ds(me, 1)] = j_send[pl.ds(zh, 1)]
        for d in range(1, 16):
            j_copy(d).start()

    def stage_j():
        for d in range(1, 16):
            j_take(d).wait_recv()
        row8 = lax.broadcasted_iota(jnp.int32, (8, HD), 0)
        rows = []
        for j in range(4):
            r = tab[SOURCE + j]
            home = lax.shift_right_logical(r, 2)
            block = j_buf[home] + j_buf[8 + home]
            block = jnp.where(row8 % 4 == (r & 3), block, 0.0)
            pair = [jnp.sum(block[4 * n : 4 * n + 4], axis=0, keepdims=True) for n in range(2)]
            rows.append(jnp.concatenate(pair, axis=1))
        attended[...] = jnp.concatenate(rows, axis=0).astype(BF16)

    def place(j):
        code = tab[PLACE + j]
        mine = jnp.minimum(code, 3)
        at = jnp.maximum(code - 8, 0)
        side, step = lax.shift_right_logical(at, 4), jnp.minimum(at & 15, steps - 1)

        def block(n, carry):
            rows = pl.ds(pl.multiple_of(n * ROWS, ROWS), ROWS)
            near = jnp.where(code < 4, own[mine, rows, :], on_buf[rows, :])
            placed[j, rows, :] = jnp.where(code < 5, near, rx[side, step, rows, :])
            return carry

        lax.fori_loop(0, 128 // ROWS, block, 0)
        pltpu.make_async_copy(placed.at[j], new_cache.at[j], out_sem.at[j]).start()

    loads[0].wait()
    for p in range(PIECES):
        migrate(0, p, True)

    on_stage[...] = own[tab[ONCHIP]]
    on_copy = remote(on_stage, on_buf, on_sem.at[0], on_sem.at[1], partner)
    on_copy.start()

    kept = {}

    def after_e():
        low, high = stage_e(kept["picked"])
        loads[1].wait()
        stage_f(low, high, 0, 16)
        send_h()

    def begin():
        kept["picked"] = stage_b()

    def first_heads():
        wait_b()
        stage_c(range(0, 4))

    def last_heads():
        stage_c(range(4, 8))

    timetable = {BEGIN: begin, FIRST: first_heads, LAST: last_heads, MERGE: stage_d, PROJECT: after_e, SPREAD: stage_h}
    for s in range(1, min(steps, 7)):
        for p in range(PIECES):
            migrate(s, p, False, old=s >= 2)
            if (s, p) in timetable:
                timetable[s, p]()

    def more(s, carry):
        for p in range(PIECES):
            migrate(s, p, False, old=True)
        return carry

    if steps > 7:
        lax.fori_loop(7, steps, more, 0)
    for p in range(PIECES):
        end_piece(p)
        if (steps, p) in timetable and steps == 6:
            timetable[steps, p]()

    on_copy.wait()
    for d in range(2):

        @pl.when(has_in(d))
        def _():
            mirror(d, steps - 2, 0, PIECES).wait()
            for p in range(PIECES):
                mirror(d, steps - 1, p, 1).wait()

    for j in range(4):
        place(j)
    for p in range(PIECES):
        shares[p].wait_send()
    for d in range(1, 16):
        a_copy(d).wait_send()
        xy_copy(b_send, b_buf, b_ss, b_rs, d, True).wait_send()
        xy_copy(h_send, h_buf, h_ss, h_rs, d, False).wait_send()
    for n in range(16):

        @pl.when(u != n)
        def _():
            d_copy(n).wait_send()

    e_copy().wait_send()
    for d in range(2):

        @pl.when(has_out(d))
        def _():
            for s in (steps - 2, steps - 1):
                for p in range(PIECES):
                    hop(d, s, p).wait_send()

    stage_j()
    for d in range(1, 16):
        j_copy(d).wait_send()
    for j in range(4):
        pltpu.make_async_copy(placed.at[j], new_cache.at[j], out_sem.at[j]).wait()


def variant(number, tab, queries, new_kv, kv_cache, o_weight):
    steps = STEPS[number]
    sem = pltpu.SemaphoreType.DMA
    vmem = pltpu.VMEM
    anywhere = pl.BlockSpec(memory_space=pl.ANY)
    smem = pl.BlockSpec(memory_space=pltpu.SMEM)
    whole = pl.BlockSpec(memory_space=pltpu.VMEM)
    return pl.pallas_call(
        functools.partial(main_kernel, steps),
        out_shape=(jax.ShapeDtypeStruct((4, 256), BF16), jax.ShapeDtypeStruct(kv_cache.shape, BF16)),
        in_specs=[smem, whole, whole, anywhere, anywhere],
        out_specs=(whole, anywhere),
        scratch_shapes=[
            vmem((4, 128, 2048), BF16),
            [vmem((4, ROWS, 2048), BF16) for _ in range(PIECES)],
            vmem((2, steps, 64, 2048), BF16),
            vmem((2, steps, 128, 2048), BF16),
            vmem((128, 2048), BF16), vmem((128, 2048), BF16),
            vmem((4, 128, 2048), BF16),
            vmem((256, 8192), BF16),
            vmem((16, HD), BF16), vmem((16, 16, HD), BF16),
            vmem((16, HD), BF16), vmem((16, 16, HD), BF16),
            vmem((16, 16, 2 * HD), F32), vmem((16, 16, 2 * HD), F32),
            vmem((16, 2 * HD), F32), vmem((16, 2 * HD), F32),
            vmem((16, 8, 256), F32), vmem((16, 8, 256), F32),
            vmem((2, 8, HD), F32), vmem((16, 8, HD), F32),
            sem((2, steps, PIECES)), sem((2, steps, PIECES)),
            sem((2, steps, PIECES)), sem((2, steps, PIECES)),
            sem((PIECES,)), sem((PIECES,)), sem((2,)), sem((2,)), sem((4,)),
            sem((15,)), sem((15,)), sem((15,)), sem((15,)), sem((16,)), sem((16,)),
            sem((2,)), sem((15,)), sem((15,)), sem((15,)), sem((15,)),
        ],
        compiler_params=pltpu.CompilerParams(
            collective_id=number, has_side_effects=True, vmem_limit_bytes=36 * 2**20
        ),
        name="migrate_and_attend",
    )(tab, queries, new_kv, kv_cache, o_weight)


def on_device(queries, new_kv, kv_cache, lengths, move_from, o_weight):
    smem = pl.BlockSpec(memory_space=pltpu.SMEM)
    words = functools.partial(pltpu.SMEM, dtype=jnp.int32)
    tab, pick = pl.pallas_call(
        plan_kernel,
        out_shape=(jax.ShapeDtypeStruct((64,), jnp.int32), jax.ShapeDtypeStruct((1,), jnp.int32)),
        in_specs=[smem, smem],
        out_specs=(smem, smem),
        scratch_shapes=[words((32,)), words((16,)), words((32,)), words((16,)), words((32,))],
        name="plan",
    )(move_from, lengths)
    branches = [functools.partial(variant, n) for n in range(len(STEPS))]
    return lax.switch(pick[0], branches, tab, queries, new_kv, kv_cache, o_weight)


def solution(mesh):
    in_specs = (P("inst", "tp"), P("inst", None), P("inst", "tp", None), P(), P(), P("tp", None))
    out_specs = (P("inst", "tp"), P("inst", "tp", None))
    return jax.shard_map(
        on_device, mesh=mesh, in_specs=in_specs, out_specs=out_specs, check_vma=False
    )
```

```python
import functools

import jax
import jax.numpy as jnp
from jax import lax
from jax.experimental import pallas as pl
from jax.experimental.pallas import tpu as pltpu
from jax.sharding import PartitionSpec as P

MESH = pl.DeviceIdType.MESH
KVH = 8
HD = 128
SCALE = HD ** -0.5
STEPS = (6, 7, 8, 9, 12)
PIECES = 4
ROWS = 16
F32 = jnp.float32
BF16 = jnp.bfloat16

BEGIN, FIRST, LAST, MERGE, PROJECT, SPREAD = (1, 2), (2, 1), (2, 2), (3, 3), (5, 1), (6, 2)

SEND, PLACE, SLOT_OF, LENGTH, SOURCE, ONCHIP, DUMP = 0, 32, 40, 44, 48, 52, 63


def plan_kernel(move_ref, len_ref, tab_ref, pick_ref, slot_of, count, rank, par, free):
    inst = lax.axis_index("inst")
    chip = inst // 2
    tab_ref[ONCHIP] = 0
    for n in range(32):
        tab_ref[SEND + n] = -1
        slot_of[move_ref[n]] = n
    for n in range(16):
        count[n] = 0
    for r in range(32):
        kind = (r // 8) * 4 + lax.shift_right_logical(slot_of[r], 3)
        seen = count[kind]
        rank[r] = seen
        count[kind] = seen + 1
    most = jnp.int32(STEPS[0])
    for d in range(2):

        def number(a, b):
            return count[a * 4 + b] if d == 0 else count[(3 - a) * 4 + 3 - b]

        n02, n03, n12, n13 = number(0, 2), number(0, 3), number(1, 2), number(1, 3)
        o0, o1 = n02 + n03, n12 + n13
        par[d * 8 + 0] = n03
        par[d * 8 + 1] = o0
        par[d * 8 + 2] = n13
        one = jnp.int32(1)
        mask = lax.shift_left(lax.shift_left(one, n03) - 1, jnp.int32(2))
        again = lax.shift_left(lax.shift_left(one, jnp.maximum(n13 - 1, 0)) - 1, o0 + 2)
        mask = mask | jnp.where(n13 > 0, again | 2, 0)
        seen = jnp.int32(0)
        for s in range(10):
            free[d * 16 + seen] = s
            seen = seen + 1 - (lax.shift_right_logical(mask, jnp.int32(s)) & 1)
        most = jnp.maximum(most, o0 + jnp.maximum(o1, jnp.minimum(o0, 1)))
        most = jnp.maximum(most, jnp.where(n13 > 1, o0 + n13 + 1, 0))
    pick = jnp.int32(0)
    for steps in STEPS[:-1]:
        pick = pick + (most > steps).astype(jnp.int32)
    pick_ref[0] = pick

    def first_step(r, a_chip, b_chip):
        d = (b_chip < a_chip).astype(jnp.int32)
        a = jnp.where(d == 1, 3 - a_chip, a_chip)
        b = jnp.where(d == 1, 3 - b_chip, b_chip)
        k = rank[r]
        n03, o0, n13 = par[d * 8], par[d * 8 + 1], par[d * 8 + 2]
        p0 = k + jnp.where(b == 3, 0, jnp.where(b == 2, n03, o0))
        q = jnp.where(b == 3, k, n13 + k)
        p1 = jnp.where(q == 0, 0, o0 + q)
        p2 = free[d * 16 + k]
        return d, jnp.where(a == 0, p0, jnp.where(a == 1, p1, p2)), b - a

    for q in range(8):
        r = chip * 8 + q
        b = lax.shift_right_logical(slot_of[r], 3)
        d, step, _ = first_step(r, chip, b)
        tab_ref[jnp.where(b == chip, DUMP, SEND + d * 16 + step)] = q
    for k in range(4):
        r = inst * 4 + k
        g = slot_of[r]
        home = lax.shift_right_logical(g, 2)
        tab_ref[jnp.where((home != inst) & (home // 2 == chip), ONCHIP, DUMP)] = k
        tab_ref[SLOT_OF + k] = g
        tab_ref[LENGTH + k] = len_ref[r]
    for j in range(4):
        r = move_ref[inst * 4 + j]
        home = lax.shift_right_logical(r, 2)
        a = lax.shift_right_logical(r, 3)
        d, step, hops = first_step(r, a, chip)
        arrival = 8 + d * 16 + step + hops - 1
        tab_ref[PLACE + j] = jnp.where(home == inst, r & 3, jnp.where(a == chip, 4, arrival))
        tab_ref[SOURCE + j] = r


def main_kernel(
    steps, tab, q_ref, new_ref, cache, weight, attended, new_cache,
    own, part, tx, rx, on_stage, on_buf, placed, w_buf,
    a_send, a_buf, b_send, b_buf, d_send, d_buf, e_send, e_buf, h_send, h_buf, j_send, j_buf,
    tx_sem, rx_sem, mir_send, mir_recv, part_send, part_recv, on_sem, load_sem, out_sem,
    a_ss, a_rs, b_ss, b_rs, d_ss, d_rs, e_sem, h_ss, h_rs, j_ss, j_rs,
):
    inst = lax.axis_index("inst")
    tp = lax.axis_index("tp")
    chip, core = inst // 2, inst % 2
    zh, u = tp % 2, tp // 2
    me = zh * 8 + inst
    partner = {"inst": chip * 2 + 1 - core}
    z_partner = {"tp": u * 2 + 1 - zh}

    def peer16(d):
        e = (me + d) % 16
        return {"inst": e % 8, "tp": u * 2 + e // 8}

    def peer_xy(d):
        return {"tp": ((u + d) % 16) * 2 + zh}

    def remote(src, dst, ss, rs, to):
        return pltpu.make_async_remote_copy(
            src_ref=src, dst_ref=dst, send_sem=ss, recv_sem=rs, device_id=to, device_id_type=MESH
        )

    half = pl.multiple_of(core * 64, 64)
    other = pl.multiple_of(64 - core * 64, 64)
    loads = [
        pltpu.make_async_copy(cache, own, load_sem.at[0]),
        pltpu.make_async_copy(weight, w_buf, load_sem.at[1]),
    ]
    for load in loads:
        load.start()

    lanes = pl.ds(pl.multiple_of((u // 2) * HD, HD), HD)
    value_lanes = pl.ds(pl.multiple_of(KVH * HD + (u // 2) * HD, HD), HD)
    q = q_ref[...].astype(F32)
    packed = jnp.concatenate(
        [q[:, :HD], q[:, HD:], new_ref[:, lanes].astype(F32), new_ref[:, value_lanes].astype(F32)], axis=0
    ).astype(BF16)
    a_send[...] = packed
    a_buf[pl.ds(me, 1)] = packed[None]

    barrier = pltpu.get_barrier_semaphore()
    for d in range(1, 16):
        pl.semaphore_signal(barrier, inc=1, device_id=peer16(d), device_id_type=MESH)
        pl.semaphore_signal(barrier, inc=1, device_id=peer_xy(d), device_id_type=MESH)
    pl.semaphore_wait(barrier, 30)

    def a_copy(d):
        return remote(a_send, a_buf.at[me], a_ss.at[d - 1], a_rs.at[d - 1], peer16(d))

    def a_take(d):
        return remote(a_send, a_buf.at[(me + 16 - d) % 16], a_ss.at[d - 1], a_rs.at[d - 1], peer16(d))

    shares = [
        remote(
            cache.at[:, pl.ds(pl.multiple_of(other + p * ROWS, ROWS), ROWS)],
            part[p], part_send.at[p], part_recv.at[p], partner,
        )
        for p in range(PIECES)
    ]
    shares[0].start()
    for d in range(1, 16):
        a_copy(d).start()
    for share in shares[1:]:
        share.start()

    def has_in(d):
        return chip > 0 if d == 0 else chip < 3

    def has_out(d):
        return chip < 3 if d == 0 else chip > 0

    def hop(d, s, p):
        to = {"inst": jnp.clip(inst + (2 if d == 0 else -2), 0, 7)}
        src = tx.at[d, s, pl.ds(p * ROWS, ROWS)]
        dst = rx.at[d, s, pl.ds(pl.multiple_of(half + p * ROWS, ROWS), ROWS)]
        return remote(src, dst, tx_sem.at[d, s, p], rx_sem.at[d, s, p], to)

    def mirror(d, s, p0, count):
        block = rx.at[d, s, pl.ds(pl.multiple_of(half + p0 * ROWS, ROWS), count * ROWS)]
        return remote(block, block, mir_send.at[d, s, p0], mir_recv.at[d, s, p0], partner)

    def migrate(s, p, first, old=False):
        rows = pl.ds(p * ROWS, ROWS)
        if first:
            shares[p].wait_recv()
        own_rows = pl.ds(pl.multiple_of(half + p * ROWS, ROWS), ROWS)
        for d in range(2):
            if not first:

                @pl.when(has_in(d))
                def _():
                    hop(d, s - 1, p).wait_recv()

            @pl.when(has_out(d))
            def _():
                code = tab[SEND + d * 16 + s]
                choice = jnp.maximum(code, 0)
                mine = lax.shift_right_logical(choice, 2) == core
                index = choice & 3
                block = jnp.where(mine, own[index, own_rows, :], part[p][index])
                if not first:
                    block = jnp.where(code < 0, rx[d, s - 1, own_rows, :], block)
                tx[d, s, rows, :] = block
                hop(d, s, p).start()
                if old:
                    hop(d, s - 2, p).wait_send()

            if not first and p == PIECES - 1:

                @pl.when(has_in(d))
                def _():
                    mirror(d, s - 1, 0, PIECES).start()
                    if old:
                        mirror(d, s - 2, 0, PIECES).wait()

    def end_piece(p):
        for d in range(2):

            @pl.when(has_in(d))
            def _():
                hop(d, steps - 1, p).wait_recv()
                mirror(d, steps - 1, p, 1).start()

    row16 = lax.broadcasted_iota(jnp.int32, (16, 1), 0)

    def by_slot(kind, values):
        out = jnp.full(kind.shape, values[0], jnp.int32)
        for k in range(1, 4):
            out = jnp.where(kind == k, values[k], out)
        return out

    def xy_copy(send, buf, ss, rs, d, whole):
        src = send if whole else send.at[(u + d) % 16]
        return remote(src, buf.at[u], ss.at[d - 1], rs.at[d - 1], peer_xy(d))

    def xy_take(send, buf, ss, rs, d, whole):
        src = send if whole else send.at[(u + d) % 16]
        return remote(src, buf.at[(u + 16 - d) % 16], ss.at[d - 1], rs.at[d - 1], peer_xy(d))

    def stage_b():
        for d in range(1, 16):
            a_take(d).wait_recv()
        blocks, spots = [], []
        for k in range(4):
            g = tab[SLOT_OF + k]
            spots.append(g & 3)
            for z in range(2):
                blocks.append(a_buf[z * 8 + lax.shift_right_logical(g, 2)])
        stacked = jnp.concatenate(blocks, axis=0)
        row = lax.broadcasted_iota(jnp.int32, (48, 128), 0)
        col = lax.broadcasted_iota(jnp.int32, (48, 128), 1)
        inner = row % 16
        k, h, group = inner // 4, inner % 4, row // 16
        spot = by_slot(k, spots)
        place = jnp.where(
            group == 0, (k * 2 + h // 2) * 16 + (h % 2) * 4, k * 32 + 4 + group * 4
        )
        chosen = (col == place + spot).astype(F32).astype(BF16)
        picked = jnp.dot(chosen, stacked, preferred_element_type=F32)
        mine = picked[:16].astype(BF16)
        b_send[...] = mine
        b_buf[pl.ds(u, 1)] = mine[None]
        for d in range(1, 16):
            xy_copy(b_send, b_buf, b_ss, b_rs, d, True).start()
        return picked

    def wait_b():
        for d in range(1, 16):
            xy_take(b_send, b_buf, b_ss, b_rs, d, True).wait_recv()

    row32 = lax.broadcasted_iota(jnp.int32, (32, 1), 0)
    of_row = (row32 % 16) // 4

    def stage_c(heads):
        limit = by_slot(of_row, [tab[LENGTH + k] for k in range(4)])
        position = tp * 128 + lax.broadcasted_iota(jnp.int32, (32, 128), 1)
        usable = position < limit
        for k in heads:
            query = b_buf[2 * k : 2 * k + 2].reshape(32, HD)
            keys = own[:, :, k * HD : (k + 1) * HD].reshape(512, HD)
            values = own[:, :, (KVH + k) * HD : (KVH + k + 1) * HD].reshape(512, HD)
            full = lax.dot_general(query, keys, (((1,), (1,)), ((), ())), preferred_element_type=F32)
            scores = full[:, :128]
            for r in range(1, 4):
                scores = jnp.where(of_row == r, full[:, r * 128 : (r + 1) * 128], scores)
            masked = jnp.where(usable, scores * SCALE, -1e30)
            top = jnp.max(masked, axis=1, keepdims=True)
            weights = jnp.where(usable, jnp.exp(masked - top), 0.0)
            total = jnp.sum(weights, axis=1, keepdims=True)
            spread = jnp.concatenate(
                [jnp.where(of_row == r, weights, 0.0).astype(BF16) for r in range(4)], axis=1
            )
            summed = jnp.dot(spread, values, preferred_element_type=F32)
            lane = lax.broadcasted_iota(jnp.int32, (32, HD), 1)
            stats = jnp.where(lane < 64, top, total)
            d_send[2 * k : 2 * k + 2] = jnp.concatenate([summed, stats], axis=1).reshape(2, 16, 2 * HD)
            for to in (2 * k, 2 * k + 1):

                @pl.when(u != to)
                def _():
                    d_copy(to).start()

                @pl.when(u == to)
                def _():
                    d_buf[to] = d_send[to]

    def d_copy(to):
        there = {"tp": to * 2 + zh}
        return remote(d_send.at[to], d_buf.at[u], d_ss.at[to], d_rs.at[u], there)

    def d_take(n):
        there = {"tp": n * 2 + zh}
        return remote(d_send.at[n], d_buf.at[n], d_ss.at[n], d_rs.at[n], there)

    def merge(blocks):
        tops = [block[:, HD : HD + 1] for block in blocks]
        top = functools.reduce(jnp.maximum, tops)
        factors = [jnp.exp(t - top) for t in tops]
        summed = sum(block[:, :HD] * f for block, f in zip(blocks, factors))
        total = sum(block[:, HD + 64 : HD + 65] * f for block, f in zip(blocks, factors))
        return top, total, summed

    def e_copy():
        return remote(e_send, e_buf, e_sem.at[0], e_sem.at[1], z_partner)

    def stage_d():
        for n in range(16):

            @pl.when(u != n)
            def _():
                d_take(n).wait_recv()

        top, total, summed = merge([d_buf[n] for n in range(16)])
        lane = lax.broadcasted_iota(jnp.int32, (16, HD), 1)
        e_send[...] = jnp.concatenate([summed, jnp.where(lane < 64, top, total)], axis=1)
        e_copy().start()

    def stage_e(picked):
        e_copy().wait_recv()
        top, total, summed = merge([e_send[...], e_buf[...]])
        query, key, value = picked[:16], picked[16:32], picked[32:48]
        own_score = jnp.sum(query * key, axis=1, keepdims=True) * SCALE
        highest = jnp.maximum(top, own_score)
        old, new = jnp.exp(top - highest), jnp.exp(own_score - highest)
        attention = ((summed * old + new * value) / (total * old + new)).astype(BF16)
        row = lax.broadcasted_iota(jnp.int32, (16, 16), 0)
        col = lax.broadcasted_iota(jnp.int32, (16, 16), 1)
        heads = []
        for h in range(2):
            chosen = ((col == (row % 4) * 4 + zh * 2 + h) & (row < 8)).astype(F32).astype(BF16)
            heads.append(jnp.dot(chosen, attention, preferred_element_type=F32))
        both = jnp.concatenate(heads, axis=1)
        low = jnp.where(row16 < 4, both, 0.0).astype(BF16)
        high = jnp.where(row16 >= 4, both, 0.0).astype(BF16)
        return low, high

    def stage_f(low, high):
        for d in (*range(1, 16), 0):
            n = (u + d) % 16
            left = w_buf[:, pl.ds(pl.multiple_of(n * 512, 512), 256)]
            right = w_buf[:, pl.ds(pl.multiple_of(n * 512 + 256, 256), 256)]
            out = jnp.dot(low, left, preferred_element_type=F32)
            out = (out + jnp.dot(high, right, preferred_element_type=F32))[:8]
            if d == 0:
                h_buf[pl.ds(u, 1)] = out[None]
            else:
                h_send[pl.ds(n, 1)] = out[None]
                xy_copy(h_send, h_buf, h_ss, h_rs, d, False).start()

    def j_copy(d):
        half_of_z = j_send.at[((me + d) % 16) // 8]
        return remote(half_of_z, j_buf.at[me], j_ss.at[d - 1], j_rs.at[d - 1], peer16(d))

    def j_take(d):
        return remote(j_send.at[0], j_buf.at[(me + 16 - d) % 16], j_ss.at[d - 1], j_rs.at[d - 1], peer16(d))

    def stage_h():
        for d in range(1, 16):
            xy_take(h_send, h_buf, h_ss, h_rs, d, False).wait_recv()
        total = sum(h_buf[n] for n in range(16))
        for z in range(2):
            rows = total[4 * z : 4 * z + 4]
            j_send[z] = jnp.concatenate([rows[:, :HD], rows[:, HD:]], axis=0)
        j_buf[pl.ds(me, 1)] = j_send[pl.ds(zh, 1)]
        for d in range(1, 16):
            j_copy(d).start()

    def stage_j():
        for d in range(1, 16):
            j_take(d).wait_recv()
        row8 = lax.broadcasted_iota(jnp.int32, (8, HD), 0)
        rows = []
        for j in range(4):
            r = tab[SOURCE + j]
            home = lax.shift_right_logical(r, 2)
            block = j_buf[home] + j_buf[8 + home]
            block = jnp.where(row8 % 4 == (r & 3), block, 0.0)
            pair = [jnp.sum(block[4 * n : 4 * n + 4], axis=0, keepdims=True) for n in range(2)]
            rows.append(jnp.concatenate(pair, axis=1))
        attended[...] = jnp.concatenate(rows, axis=0).astype(BF16)

    def place(j):
        code = tab[PLACE + j]
        mine = jnp.minimum(code, 3)
        at = jnp.maximum(code - 8, 0)
        side, step = lax.shift_right_logical(at, 4), jnp.minimum(at & 15, steps - 1)

        def block(n, carry):
            rows = pl.ds(pl.multiple_of(n * ROWS, ROWS), ROWS)
            near = jnp.where(code < 4, own[mine, rows, :], on_buf[rows, :])
            placed[j, rows, :] = jnp.where(code < 5, near, rx[side, step, rows, :])
            return carry

        lax.fori_loop(0, 128 // ROWS, block, 0)
        pltpu.make_async_copy(placed.at[j], new_cache.at[j], out_sem.at[j]).start()

    loads[0].wait()
    for p in range(PIECES):
        migrate(0, p, True)

    on_stage[...] = own[tab[ONCHIP]]
    on_copy = remote(on_stage, on_buf, on_sem.at[0], on_sem.at[1], partner)
    on_copy.start()

    kept = {}

    def after_e():
        low, high = stage_e(kept["picked"])
        loads[1].wait()
        stage_f(low, high)

    def begin():
        kept["picked"] = stage_b()

    def first_heads():
        wait_b()
        stage_c(range(0, 4))

    def last_heads():
        stage_c(range(4, 8))

    timetable = {BEGIN: begin, FIRST: first_heads, LAST: last_heads, MERGE: stage_d, PROJECT: after_e, SPREAD: stage_h}
    for s in range(1, min(steps, 7)):
        for p in range(PIECES):
            migrate(s, p, False, old=s >= 2)
            if (s, p) in timetable:
                timetable[s, p]()

    def more(s, carry):
        for p in range(PIECES):
            migrate(s, p, False, old=True)
        return carry

    if steps > 7:
        lax.fori_loop(7, steps, more, 0)
    for p in range(PIECES):
        end_piece(p)
        if (steps, p) in timetable and steps == 6:
            timetable[steps, p]()

    on_copy.wait()
    for d in range(2):

        @pl.when(has_in(d))
        def _():
            mirror(d, steps - 2, 0, PIECES).wait()
            for p in range(PIECES):
                mirror(d, steps - 1, p, 1).wait()

    for j in range(4):
        place(j)
    for p in range(PIECES):
        shares[p].wait_send()
    for d in range(1, 16):
        a_copy(d).wait_send()
        xy_copy(b_send, b_buf, b_ss, b_rs, d, True).wait_send()
        xy_copy(h_send, h_buf, h_ss, h_rs, d, False).wait_send()
    for n in range(16):

        @pl.when(u != n)
        def _():
            d_copy(n).wait_send()

    e_copy().wait_send()
    for d in range(2):

        @pl.when(has_out(d))
        def _():
            for s in (steps - 2, steps - 1):
                for p in range(PIECES):
                    hop(d, s, p).wait_send()

    stage_j()
    for d in range(1, 16):
        j_copy(d).wait_send()
    for j in range(4):
        pltpu.make_async_copy(placed.at[j], new_cache.at[j], out_sem.at[j]).wait()


def variant(number, tab, queries, new_kv, kv_cache, o_weight):
    steps = STEPS[number]
    sem = pltpu.SemaphoreType.DMA
    vmem = pltpu.VMEM
    anywhere = pl.BlockSpec(memory_space=pl.ANY)
    smem = pl.BlockSpec(memory_space=pltpu.SMEM)
    whole = pl.BlockSpec(memory_space=pltpu.VMEM)
    return pl.pallas_call(
        functools.partial(main_kernel, steps),
        out_shape=(jax.ShapeDtypeStruct((4, 256), BF16), jax.ShapeDtypeStruct(kv_cache.shape, BF16)),
        in_specs=[smem, whole, whole, anywhere, anywhere],
        out_specs=(whole, anywhere),
        scratch_shapes=[
            vmem((4, 128, 2048), BF16),
            [vmem((4, ROWS, 2048), BF16) for _ in range(PIECES)],
            vmem((2, steps, 64, 2048), BF16),
            vmem((2, steps, 128, 2048), BF16),
            vmem((128, 2048), BF16), vmem((128, 2048), BF16),
            vmem((4, 128, 2048), BF16),
            vmem((256, 8192), BF16),
            vmem((16, HD), BF16), vmem((16, 16, HD), BF16),
            vmem((16, HD), BF16), vmem((16, 16, HD), BF16),
            vmem((16, 16, 2 * HD), F32), vmem((16, 16, 2 * HD), F32),
            vmem((16, 2 * HD), F32), vmem((16, 2 * HD), F32),
            vmem((16, 8, 256), F32), vmem((16, 8, 256), F32),
            vmem((2, 8, HD), F32), vmem((16, 8, HD), F32),
            sem((2, steps, PIECES)), sem((2, steps, PIECES)),
            sem((2, steps, PIECES)), sem((2, steps, PIECES)),
            sem((PIECES,)), sem((PIECES,)), sem((2,)), sem((2,)), sem((4,)),
            sem((15,)), sem((15,)), sem((15,)), sem((15,)), sem((16,)), sem((16,)),
            sem((2,)), sem((15,)), sem((15,)), sem((15,)), sem((15,)),
        ],
        compiler_params=pltpu.CompilerParams(
            collective_id=number, has_side_effects=True, vmem_limit_bytes=36 * 2**20
        ),
        name="migrate_and_attend",
    )(tab, queries, new_kv, kv_cache, o_weight)


def on_device(queries, new_kv, kv_cache, lengths, move_from, o_weight):
    smem = pl.BlockSpec(memory_space=pltpu.SMEM)
    words = functools.partial(pltpu.SMEM, dtype=jnp.int32)
    tab, pick = pl.pallas_call(
        plan_kernel,
        out_shape=(jax.ShapeDtypeStruct((64,), jnp.int32), jax.ShapeDtypeStruct((1,), jnp.int32)),
        in_specs=[smem, smem],
        out_specs=(smem, smem),
        scratch_shapes=[words((32,)), words((16,)), words((32,)), words((16,)), words((32,))],
        name="plan",
    )(move_from, lengths)
    branches = [functools.partial(variant, n) for n in range(len(STEPS))]
    return lax.switch(pick[0], branches, tab, queries, new_kv, kv_cache, o_weight)


def solution(mesh):
    in_specs = (P("inst", "tp"), P("inst", None), P("inst", "tp", None), P(), P(), P("tp", None))
    out_specs = (P("inst", "tp"), P("inst", "tp", None))
    return jax.shard_map(
        on_device, mesh=mesh, in_specs=in_specs, out_specs=out_specs, check_vma=False
    )
```
